32 devices in a mesh: dp: 8 (over z, y), tensor: 4 (over x, core).
Axes of the slice: x: 2, y: 2, z: 4, core: 2. Of those that a mesh axis runs over, the one named last changes fastest.
Arguments:
- tokens: bfloat16 [8192, 1024], P('dp'), may hold values from -6 to 6
- positions: int32 [8192], P('dp'), may hold values from 0 to 1023, as said below
- routes: int32 [8192, 8], P('dp'), may hold values from 0 to 31, all different within a row; in each aligned block of 1024 rows (0 to 1023, 1024 to 2047, ...) at most 384 rows name the same one
- gates: float32 [8192, 8], P('dp'), may hold values from 0.06 to 0.19
- norm1_gain: float32 [1024], replicated, may hold values from 0.5 to 1.5
- w_query: bfloat16 [1024, 1024], P(None, 'tensor'), may hold values from -0.25 to 0.25
- w_key: bfloat16 [1024, 512], P(None, 'tensor'), may hold values from -0.25 to 0.25
- w_value: bfloat16 [1024, 512], P(None, 'tensor'), may hold values from -0.1875 to 0.1875
- w_out: bfloat16 [1024, 1024], P('tensor'), may hold values from -0.75 to 0.75
- norm2_gain: float32 [1024], replicated, may hold values from 0.5 to 1.5
- w_gate: bfloat16 [32, 1024, 512], P(None, None, 'tensor'), may hold values from -0.1875 to 0.1875
- w_up: bfloat16 [32, 1024, 512], P(None, None, 'tensor'), may hold values from -0.1875 to 0.1875
- w_down: bfloat16 [32, 512, 1024], P(None, 'tensor'), may hold values from -0.75 to 0.75
- out_grad: bfloat16 [8192, 1024], P('dp'), may hold values from -6 to 6
Outputs:
- block_out: float32 [8192, 1024], P('dp')
- tokens_grad: float32 [8192, 1024], P('dp')
- grad_norm1_gain: float32 [1024], P('dp')
- grad_w_query: float32 [1024, 1024], P('dp', 'tensor')
- grad_w_key: float32 [1024, 512], P('dp', 'tensor')
- grad_w_value: float32 [1024, 512], P('dp', 'tensor')
- grad_w_out: float32 [1024, 1024], P('tensor', 'dp')
- grad_norm2_gain: float32 [1024], P('dp')
- grad_w_gate: float32 [32, 1024, 512], P(None, 'dp', 'tensor')
- grad_w_up: float32 [32, 1024, 512], P(None, 'dp', 'tensor')
- grad_w_down: float32 [32, 512, 1024], P(None, 'tensor', 'dp')
The draws below stay inside these ranges and needn't reach their ends.
Inputs may be any that keep to these rules, and one draw needn't show every extreme that they name: Within each sequence of 1024 rows positions count up by one and start again at 0 where a new document begins; the first row of each sequence begins a document; in every draw some sequence is one whole document. `routes`: A token names 8 different experts; in the 1024 rows of one device no expert is named by more than 384 rows, and in every draw some expert is named by exactly 384 rows of some device.
All inputs are finite; a program needn't handle non-finite values.
Results may differ from the reference program's by a relative error of at most 0.014.
Values sent between devices are 32-bit elements; how exact they have to be, the bound alone decides.
No kernel may reach another device: no remote copies, remote signals or barrier semaphores. Data moves between devices by JAX's collectives and lax.ppermute only.
A program may use at most 384 MiB of HBM per device.

```python
import math
import jax
import jax.numpy as jnp
import numpy as np
from jax import lax

D = 1024
HEADS = 16
KV_HEADS = 8
HEAD_DIM = 64
FF = 512
EXPERTS = 32
TOP = 8
TOK_DEV = 1024
CAP = 384
TOKENS = 8192


def draw_positions(key, part):
    key = jax.random.fold_in(key, 7)
    start_key, whole_key = jax.random.split(key)
    seq_total = TOKENS // TOK_DEV
    whole_seq = jax.random.randint(whole_key, (), 0, seq_total)
    starts = jax.random.randint(start_key, (TOKENS,), 0, 192) == 0
    flat_index = jnp.arange(TOKENS, dtype=jnp.int32)
    row_index = flat_index % TOK_DEV
    seq_index = flat_index // TOK_DEV
    starts = starts & (seq_index != whole_seq) | (row_index == 0)
    marked = jnp.where(starts, row_index, 0).reshape(seq_total, TOK_DEV)
    latest = lax.cummax(marked, axis=1).reshape(TOKENS)
    return (row_index - latest).astype(jnp.int32)


def raised(drawn, key, source, target, shards_of, factor):
    owner, partner = [(jnp.arange(drawn.shape[position]) // (drawn.shape[position] // shards_of)).reshape([-1 if axis == position else 1 for axis in range(drawn.ndim)]) for position in (source, target)]
    chosen = jax.random.permutation(key, shards_of)[partner]
    strong = (owner == chosen) | (owner == (partner + shards_of // 2) % shards_of)
    return jnp.where(strong, factor * drawn, drawn)


def block_levels(own_key, dims, cuts, least, top_value):
    factor_of = 1.0
    for position, shards_of in cuts:
        steps = jax.random.uniform(jax.random.fold_in(jax.random.fold_in(own_key, 6), position), (shards_of,), jnp.float32, least / len(cuts), top_value / len(cuts))
        factor_of = factor_of * jnp.repeat(jnp.exp(steps), dims[position] // shards_of).reshape((-1,) + (1,) * (len(dims) - 1 - position))
    return factor_of


def assign_block(key, own, number, rows, number_of, top, bound, slope):
    order = jax.random.permutation(key, number_of)
    heavy_load, ordinary = load_shares(number_of, rows * top, bound, slope, True), load_shares(number_of, rows * top, bound, slope, False)
    places = jnp.arange(number_of)

    def named(lengths, turn):
        used = int((lengths > 0).sum())
        fixed = max(1, used // 4)
        moved = fixed + (places - fixed + turn * (used - fixed)) % max(1, number_of - fixed)
        return jnp.zeros((number_of,), jnp.int32).at[order[jnp.where(places < fixed, places, moved)]].set(jnp.asarray(lengths, jnp.int32))

    lengths = jnp.where(number % 4 == 0, named(heavy_load, number // 4), named(ordinary, number - number // 4 - 1))
    mixed = jax.random.permutation(jax.random.fold_in(own, 3), number_of)
    source_of, taker = mixed[0:number_of // 2 * 2:2], mixed[1:number_of // 2 * 2:2]
    slack = jnp.minimum(lengths[source_of] - 1, bound - lengths[taker]) // 2
    slack = jnp.where((source_of == order[0]) | (taker == order[0]) | (lengths[taker] == 0), 0, jnp.maximum(slack, 0))
    moved = jax.random.randint(jax.random.fold_in(own, 4), (number_of // 2,), 0, 1 << 20) % (slack + 1)
    lengths = lengths.at[source_of].add(-moved).at[taker].add(moved)
    labels = jnp.searchsorted(jnp.cumsum(lengths), jnp.arange(rows * top), side="right").astype(jnp.int32)
    listing = labels.reshape(top, rows).T
    listing = listing[jax.random.permutation(jax.random.fold_in(own, 1), rows)]
    turn = jax.random.randint(jax.random.fold_in(own, 2), (rows, 1), 0, top)
    return jnp.take_along_axis(listing, (jnp.arange(top)[None, :] + turn) % top, axis=1)


def load_shares(number_of, total, limit, slope, full):
    weights = [(1 << 20) // math.isqrt(standing ** slope) + 1 for standing in range(1, number_of + 1)]
    largest = limit if full else min(limit, max(-(-total // number_of), total * weights[0] // sum(weights)))
    least = 1 if total - largest >= number_of - 1 else 0
    holding, rest = [largest] + [least] * (number_of - 1), total - largest - least * (number_of - 1)
    while rest > 0:
        candidates = [i for i in range(1, number_of) if holding[i] < largest] or [i for i in range(1, number_of) if holding[i] < limit]
        whole, remaining = sum([weights[i] for i in candidates]), rest
        for i in candidates:
            addition = min(limit - holding[i], max(1, remaining * weights[i] // whole), rest)
            holding[i] = holding[i] + addition
            rest = rest - addition
    return np.array(holding)


def scatter_about(rng, shape, deviation, reach, cuts=(), kind=jnp.bfloat16):
    values = jax.random.normal(rng, shape, jnp.float32) * deviation
    if len(cuts) > 0:
        values = block_levels(rng, shape, cuts, -0.22, 0.18) * values
    return jnp.clip(values, min=-reach, max=reach).astype(kind)


def bell_draw_with(own_key, dims, width, limit, cuts, heavy, kind=jnp.bfloat16):
    values = width * jax.random.normal(own_key, dims, jnp.float32)
    if cuts:
        values = values * block_levels(own_key, dims, cuts, -0.22, 0.18)
    return jnp.clip(raised(values, jax.random.fold_in(own_key, 3), *heavy), -limit, limit).astype(kind)


def setup_inputs(seed: int = 0) -> dict:
    key_list = jax.random.split(jax.random.key(seed), 15)
    tokens = scatter_about(key_list[0], (TOKENS, D), 1.0, 6.0, ((0, 8),))
    positions = draw_positions(jax.random.fold_in(key_list[14], 71), 0)
    routes_keys = jax.random.split(jax.random.fold_in(key_list[2], 1), TOKENS // TOK_DEV)
    routes_turns = jax.random.permutation(jax.random.fold_in(key_list[2], 3), TOKENS // TOK_DEV)
    routes = jax.vmap(lambda own, number: assign_block(jax.random.fold_in(key_list[2], 2), own, number, TOK_DEV, EXPERTS, TOP, CAP, 1))(routes_keys, routes_turns).reshape((TOKENS, TOP))
    gates = jnp.clip(0.06 + 0.13 * jax.random.uniform(key_list[3], (TOKENS, TOP), jnp.float32) ** block_levels(key_list[3], (TOKENS, TOP), ((0, 8),), -0.2, 0.2), 0.06, 0.19)
    norm1_gain = jnp.clip(1.0 + 0.1 * jax.random.normal(key_list[4], (D,), jnp.float32), 0.5, 1.5)
    w_query = scatter_about(key_list[5], (D, HEADS * HEAD_DIM), (D // 2) ** -0.5, 0.25, ((1, 4),))
    w_key = scatter_about(key_list[6], (D, KV_HEADS * HEAD_DIM), (D // 2) ** -0.5, 0.25, ((1, 4),))
    w_value = scatter_about(key_list[7], (D, KV_HEADS * HEAD_DIM), D ** -0.5, 0.1875, ((1, 4),))
    w_out = scatter_about(key_list[8], (HEADS * HEAD_DIM, D), (HEADS * HEAD_DIM // 16) ** -0.5, 0.75, ((0, 4),))
    norm2_gain = jnp.clip(1.0 + 0.1 * jax.random.normal(key_list[9], (D,), jnp.float32), 0.5, 1.5)
    w_gate = scatter_about(key_list[10], (EXPERTS, D, FF), D ** -0.5, 0.1875, ((2, 4),))
    w_up = scatter_about(key_list[11], (EXPERTS, D, FF), D ** -0.5, 0.1875, ((2, 4),))
    w_down = scatter_about(key_list[12], (EXPERTS, FF, D), (FF // 8) ** -0.5, 0.75, ((1, 4),))
    out_grad = bell_draw_with(key_list[13], (TOKENS, D), 1.0, 6.0, ((0, 8),), (0, 1, 8, 2.0))
    return dict(tokens=tokens, positions=positions, routes=routes, gates=gates, norm1_gain=norm1_gain, w_query=w_query, w_key=w_key, w_value=w_value, w_out=w_out, norm2_gain=norm2_gain, w_gate=w_gate, w_up=w_up, w_down=w_down, out_grad=out_grad)


EPS = 1e-06
ROPE_BASE = 10000.0
HIGH = lax.Precision.HIGHEST

@jax.custom_vjp
def low(v):
    return lax.optimization_barrier(v.astype(jnp.bfloat16)).astype(jnp.float32)

@jax.custom_vjp
def low_back(v):
    return v

def low_keep(v):
    return (low(v), None)

def low_pass(kept, grad):
    return (grad,)

def back_keep(v):
    return (v, None)

def back_low(kept, grad):
    return (low(grad),)
low.defvjp(low_keep, low_pass)
low_back.defvjp(back_keep, back_low)

def rms_norm(values_in, gain_in):
    return values_in * lax.rsqrt(lax.optimization_barrier(jnp.mean(values_in * values_in, -1, keepdims=True)) + EPS) * gain_in

def rope_tables(positions):
    half_dim = HEAD_DIM // 2
    freqs = ROPE_BASE ** (-(jnp.arange(half_dim, dtype=jnp.float32) * 2.0) / HEAD_DIM)
    angles = positions.astype(jnp.float32)[:, None] * freqs[None, :]
    cosine = jnp.cos(angles)
    sine_table = jnp.sin(angles)
    return (jnp.concatenate([cosine, cosine], -1), jnp.concatenate([sine_table, sine_table], -1))

def rotate(values_in, cosine, sine_table):
    half_dim = values_in.shape[-1] // 2
    turned = jnp.concatenate([-values_in[..., half_dim:], values_in[..., :half_dim]], -1)
    return values_in * cosine[:, None, :] + turned * sine_table[:, None, :]

def attend_one(pieces):
    query, keys_in, values_in, positions = pieces
    per_group = HEADS // KV_HEADS
    keys_all = jnp.repeat(keys_in, per_group, axis=1)
    values_all = jnp.repeat(values_in, per_group, axis=1)
    row_index = jnp.arange(TOK_DEV, dtype=jnp.int32)
    place_gap = positions[:, None] - positions[None, :]
    allowed = (row_index[:, None] >= row_index[None, :]) & (place_gap == row_index[:, None] - row_index[None, :])
    scores = low_back(jnp.einsum('qhd,khd->hqk', query, keys_all, precision=HIGH) * HEAD_DIM ** (-0.5))
    scores = jnp.where(allowed[None], scores, -1e+30)
    row_max = lax.optimization_barrier(jnp.max(scores, -1, keepdims=True))
    exp_scores = jnp.exp(scores - row_max)
    soft = exp_scores / lax.optimization_barrier(jnp.sum(exp_scores, -1, keepdims=True))
    soft_low = low(soft)
    return jnp.einsum('hqk,khd->qhd', soft_low, values_all, precision=HIGH)

def experts(normed2, routes, gates, w_gate, w_up, w_down, slot_room):
    row_count = normed2.shape[0]
    chosen = routes.reshape(-1).astype(jnp.int32)
    onehot = (chosen[:, None] == jnp.arange(EXPERTS, dtype=jnp.int32)[None, :]).astype(jnp.int32)
    before = jnp.cumsum(onehot, 0) - onehot
    slot_rank = lax.optimization_barrier(jnp.sum(before * onehot, 1))
    target = (chosen * slot_room + slot_rank).astype(jnp.int32)
    source = (jnp.arange(row_count * TOP, dtype=jnp.int32) // TOP).astype(jnp.int32)
    slot_owner = jnp.zeros((EXPERTS * slot_room,), jnp.int32).at[target].set(source)
    filled = jnp.zeros((EXPERTS * slot_room,), jnp.float32).at[target].set(1.0)
    sent_rows = (normed2[slot_owner] * filled[:, None]).reshape(EXPERTS, slot_room, D)
    gate_part = low_back(jnp.einsum('ecd,edf->ecf', sent_rows, w_gate, precision=HIGH))
    up_part = low_back(jnp.einsum('ecd,edf->ecf', sent_rows, w_up, precision=HIGH))
    active = low(jax.nn.silu(gate_part) * up_part)
    result = low_back(jnp.einsum('ecf,efd->ecd', active, w_down, precision=HIGH)).reshape(EXPERTS * slot_room, D)
    picked = result[target].reshape(row_count, TOP, D)
    return lax.optimization_barrier(jnp.sum(gates[..., None] * picked, 1))

def layer_group(params, pieces):
    gain1, w_query, w_key, w_value, w_out, gain2, w_gate, w_up, w_down = params
    token_rows, positions, routes, gates = pieces
    seq_count = token_rows.shape[0] // TOK_DEV
    normed1 = low(rms_norm(token_rows, gain1))
    query = low_back(jnp.dot(normed1, w_query, precision=HIGH))
    keys_proj = low_back(jnp.dot(normed1, w_key, precision=HIGH))
    values_low = low(low_back(jnp.dot(normed1, w_value, precision=HIGH)))
    cosine, sine_table = rope_tables(positions)
    query = low(rotate(query.reshape(-1, HEADS, HEAD_DIM), cosine, sine_table))
    keys_low = low(rotate(keys_proj.reshape(-1, KV_HEADS, HEAD_DIM), cosine, sine_table))
    mixed = lax.map(jax.checkpoint(attend_one), (query.reshape(seq_count, TOK_DEV, HEADS, HEAD_DIM), keys_low.reshape(seq_count, TOK_DEV, KV_HEADS, HEAD_DIM), values_low.reshape(seq_count, TOK_DEV, KV_HEADS, HEAD_DIM), positions.reshape(seq_count, TOK_DEV)))
    mixed = low(low_back(mixed.reshape(-1, HEADS * HEAD_DIM)))
    hidden = token_rows + low_back(jnp.dot(mixed, w_out, precision=HIGH))
    normed2 = low(rms_norm(hidden, gain2))
    return hidden + experts(normed2, routes, gates, w_gate, w_up, w_down, seq_count * CAP)

def reference(tokens, positions, routes, gates, norm1_gain, w_query, w_key, w_value, w_out, norm2_gain, w_gate, w_up, w_down, out_grad):
    params = (norm1_gain.astype(jnp.float32), w_query.astype(jnp.float32), w_key.astype(jnp.float32), w_value.astype(jnp.float32), w_out.astype(jnp.float32), norm2_gain.astype(jnp.float32), w_gate.astype(jnp.float32), w_up.astype(jnp.float32), w_down.astype(jnp.float32))
    group_seqs = math.gcd(TOKENS // TOK_DEV, max(1, 4096 // TOK_DEV))
    step_count = TOKENS // (group_seqs * TOK_DEV)
    place_blocks = positions.astype(jnp.int32).reshape(step_count, -1)
    route_blocks = routes.astype(jnp.int32).reshape(step_count, -1, TOP)
    gate_blocks = gates.astype(jnp.float32).reshape(step_count, -1, TOP)

    def forward(tokens_in, weights_in):

        def one_step(carried, block_item):
            return (carried, jax.checkpoint(layer_group)(weights_in, block_item))
        _, produced = lax.scan(one_step, jnp.zeros((), jnp.float32), (tokens_in.reshape(step_count, -1, D), place_blocks, route_blocks, gate_blocks))
        return produced.reshape(TOKENS, D)
    block_out, pullback = jax.vjp(forward, tokens.astype(jnp.float32), params)
    tokens_grad, grads = pullback(out_grad.astype(jnp.float32))
    return (block_out, tokens_grad, grads[0], grads[1], grads[2], grads[3], grads[4], grads[5], grads[6], grads[7], grads[8])
```

```python
import functools

import jax
import jax.numpy as jnp
from jax import lax
from jax.experimental import pallas as pl
from jax.experimental.pallas import tpu as pltpu
from jax.sharding import PartitionSpec as P

HEAD_DIM = 64
EXPERTS = 32
TOP = 8
EPS = 1e-06
ROPE_BASE = 10000.0
CHUNKS = 4
ROWS = 512

bfloat = jnp.bfloat16
wide = jnp.float32

CORE_PAIRS = [(i, i ^ 1) for i in range(4)]
X_PAIRS = [(i, i ^ 2) for i in range(4)]


def dot_nn(a, b):
    return jnp.dot(a, b, preferred_element_type=wide)


def dot_nt(a, b):
    return lax.dot_general(a, b, (((1,), (1,)), ((), ())), preferred_element_type=wide)


def norm_forward(v, gain):
    return v * lax.rsqrt(jnp.mean(v * v, -1, keepdims=True) + EPS) * gain


def norm_backward(v, gain, q):
    r = lax.rsqrt(jnp.mean(v * v, -1, keepdims=True) + EPS)
    gq = gain * q
    v_grad = r * gq - v * (r * r * r) * jnp.mean(v * gq, -1, keepdims=True)
    return v_grad, jnp.sum(q * v * r, 0)


def rope_tables(positions):
    half_dim = HEAD_DIM // 2
    freqs = ROPE_BASE ** (-(jnp.arange(half_dim, dtype=jnp.float32) * 2.0) / HEAD_DIM)
    angles = positions.astype(jnp.float32)[:, None] * freqs[None, :]
    cosine = jnp.cos(angles)
    sine_table = jnp.sin(angles)
    return (jnp.concatenate([cosine, cosine], -1), jnp.concatenate([sine_table, sine_table], -1))


def rotate(values_in, cosine, sine_table):
    half_dim = values_in.shape[-1] // 2
    turned = jnp.concatenate([-values_in[..., half_dim:], values_in[..., :half_dim]], -1)
    return values_in * cosine[:, None, :] + turned * sine_table[:, None, :]


def expert_parts(x, og, gate_cols, w_pair, wd2):
    hidden = wd2.shape[0] // 2
    back = dot_nt(og, wd2)
    out = []
    for j in range(2):
        both = dot_nn(x, w_pair[j])
        gate, up = both[:, :hidden], both[:, hidden:]
        col = gate_cols[j]
        sig = 0.5 * jnp.tanh(0.5 * gate) + 0.5
        act = gate * sig
        slope = sig + act * (1.0 - sig)
        weighted = back[:, j * hidden : (j + 1) * hidden] * col
        out.append(
            (
                (act * up * col).astype(bfloat),
                (weighted * up * slope).astype(bfloat),
                (weighted * act).astype(bfloat),
            )
        )
    return out


def gate_columns(g, first):
    lane = lax.broadcasted_iota(jnp.int32, g.shape, 1)
    return [
        jnp.sum(jnp.where(lane == first + j, g, 0.0), axis=1, keepdims=True) for j in range(2)
    ]


def own_body(x_ref, og_ref, g_ref, wg_ref, wu_ref, wd_ref, ga_ref, gg_ref, ug_ref, n_ref):
    pair = pl.program_id(0)
    hidden = wg_ref.shape[2]

    @pl.when(pair == 0)
    def _():
        n_ref[...] = jnp.zeros_like(n_ref)

    w_pair = [jnp.concatenate([wg_ref[j], wu_ref[j]], axis=1) for j in range(2)]
    wd2 = wd_ref[...].reshape(2 * hidden, wd_ref.shape[2])
    cols = gate_columns(g_ref[...], 2 * pair)
    parts = expert_parts(x_ref[...], og_ref[...], cols, w_pair, wd2)
    total = n_ref[...]
    for j in range(2):
        ga, gg, ug = parts[j]
        lanes = slice(j * hidden, (j + 1) * hidden)
        ga_ref[:, lanes] = ga
        gg_ref[:, lanes] = gg
        ug_ref[:, lanes] = ug
        total = total + dot_nt(jnp.concatenate([gg, ug], axis=1), w_pair[j])
    n_ref[...] = total


def own_experts(x, og, g, w_gate, w_up, w_down):
    rows, width = x.shape
    experts, _, hidden = w_gate.shape
    full = lambda shape: pl.BlockSpec(shape, lambda p: (0, 0), pipeline_mode=pl.Buffered(1))
    act_shape = jax.ShapeDtypeStruct((rows, experts * hidden), bfloat)
    act_spec = pl.BlockSpec((rows, 2 * hidden), lambda p: (0, p))
    up_spec = pl.BlockSpec((2, width, hidden), lambda p: (p, 0, 0))
    return pl.pallas_call(
        own_body,
        grid=(experts // 2,),
        in_specs=[
            full((rows, width)),
            full((rows, width)),
            full((rows, experts)),
            up_spec,
            up_spec,
            pl.BlockSpec((2, hidden, width), lambda p: (p, 0, 0)),
        ],
        out_specs=[act_spec, act_spec, act_spec, pl.BlockSpec((rows, width), lambda p: (0, 0))],
        out_shape=[act_shape, act_shape, act_shape, jax.ShapeDtypeStruct((rows, width), wide)],
        compiler_params=pltpu.CompilerParams(
            dimension_semantics=("arbitrary",), vmem_limit_bytes=48 * 2**20
        ),
        cost_estimate=pl.CostEstimate(
            flops=10 * rows * width * experts * hidden,
            bytes_accessed=6 * experts * width * hidden + 6 * rows * experts * hidden,
            transcendentals=rows * experts * hidden,
        ),
        name="own_experts",
    )(x, og, g, w_gate, w_up, w_down)


def grads_body(
    first, other_rows,
    x_ref, og_ref, g_ref, xt_ref, ogt_ref,
    ga0_ref, gg0_ref, ug0_ref, ga1_ref, gg1_ref, ug1_ref,
    wg_ref, wu_ref, wd_ref,
    keep_g, send_g, keep_u, send_u, keep_d, send_d,
    s0_ref, s1_ref, sa_ref,
):
    pair = pl.program_id(0)
    hidden = wg_ref.shape[2]
    w_pair = [jnp.concatenate([wg_ref[j], wu_ref[j]], axis=1) for j in range(2)]
    wd2 = wd_ref[...].reshape(2 * hidden, wd_ref.shape[2])
    s_refs = (s0_ref, s1_ref)

    def block(i, _):
        rows = pl.ds(pl.multiple_of(i * ROWS, ROWS), ROWS)
        cols = gate_columns(g_ref[rows, :], 2 * (pair + first))
        parts = expert_parts(x_ref[rows, :], og_ref[rows, :], cols, w_pair, wd2)
        for j in range(2):
            ga, gg, ug = parts[j]
            lanes = slice(j * hidden, (j + 1) * hidden)
            sa_ref[rows, lanes] = ga
            s_refs[j][rows, :hidden] = gg
            s_refs[j][rows, hidden:] = ug
        return 0

    lax.fori_loop(0, other_rows // ROWS, block, 0)
    half = ga0_ref.shape[0]
    for own, (ga_ref, gg_ref, ug_ref) in enumerate(
        ((ga0_ref, gg0_ref, ug0_ref), (ga1_ref, gg1_ref, ug1_ref))
    ):
        rows = slice(other_rows + own * half, other_rows + (own + 1) * half)
        sa_ref[rows, :] = ga_ref[...]
        for j in range(2):
            lanes = slice(j * hidden, (j + 1) * hidden)
            s_refs[j][rows, :hidden] = gg_ref[:, lanes]
            s_refs[j][rows, hidden:] = ug_ref[:, lanes]
    shard = xt_ref.shape[0] // 2
    for j in range(2):
        grad = dot_nn(xt_ref[...], s_refs[j][...])
        keep_g[j] = grad[:shard, :hidden]
        send_g[j] = grad[shard:, :hidden]
        keep_u[j] = grad[:shard, hidden:]
        send_u[j] = grad[shard:, hidden:]
    down = dot_nn(ogt_ref[...], sa_ref[...])
    for j in range(2):
        turned = down[:, j * hidden : (j + 1) * hidden].T
        keep_d[j] = turned[:, :shard]
        send_d[j] = turned[:, shard:]


def expert_grads(chunk, x, og, g, xt, ogt, own0, own1, w_gate, w_up, w_down):
    other_rows, width = x.shape
    experts, _, hidden = w_gate.shape
    half = own0[0].shape[0]
    total_rows = other_rows + 2 * half
    shard = xt.shape[0] // 2
    count = experts // CHUNKS
    first = chunk * count // 2
    full = lambda a: pl.BlockSpec(a.shape, lambda p: (0, 0), pipeline_mode=pl.Buffered(1))
    own_spec = pl.BlockSpec((half, 2 * hidden), lambda p: (0, p + first))
    up_spec = pl.BlockSpec((2, width, hidden), lambda p: (p + first, 0, 0))
    out_spec = pl.BlockSpec((2, shard, hidden), lambda p: (p, 0, 0))
    down_spec = pl.BlockSpec((2, hidden, shard), lambda p: (p, 0, 0))
    up_shape = jax.ShapeDtypeStruct((count, shard, hidden), wide)
    down_shape = jax.ShapeDtypeStruct((count, hidden, shard), wide)
    return pl.pallas_call(
        functools.partial(grads_body, first, other_rows),
        grid=(count // 2,),
        in_specs=[full(x), full(og), full(g), full(xt), full(ogt)]
        + [own_spec] * 6
        + [up_spec, up_spec, pl.BlockSpec((2, hidden, width), lambda p: (p + first, 0, 0))],
        out_specs=[out_spec] * 4 + [down_spec] * 2,
        out_shape=[up_shape] * 4 + [down_shape] * 2,
        scratch_shapes=[pltpu.VMEM((total_rows, 2 * hidden), bfloat)] * 3,
        compiler_params=pltpu.CompilerParams(
            dimension_semantics=("arbitrary",), vmem_limit_bytes=56 * 2**20
        ),
        cost_estimate=pl.CostEstimate(
            flops=6 * other_rows * width * count * hidden + 12 * total_rows * shard * count * hidden,
            bytes_accessed=4 * other_rows * width + 6 * count * width * hidden,
            transcendentals=other_rows * count * hidden,
        ),
        name="expert_grads",
    )(x, og, g, xt, ogt, *own0, *own1, w_gate, w_up, w_down)


def per_device(
    dp_size,
    tokens,
    positions,
    routes,
    gates,
    norm1_gain,
    w_query,
    w_key,
    w_value,
    w_out,
    norm2_gain,
    w_gate,
    w_up,
    w_down,
    out_grad,
):
    row_count, width = tokens.shape
    half = row_count // 2
    local_heads = w_query.shape[1] // HEAD_DIM
    local_groups = w_key.shape[1] // HEAD_DIM
    per_group = local_heads // local_groups
    scale_factor = HEAD_DIM ** (-0.5)
    block_rows = min(512, row_count)
    block_count = row_count // block_rows
    core = lax.axis_index("tensor") % 2
    x_side = lax.axis_index("tensor") // 2
    dp_place = lax.axis_index("dp")
    small = dp_size == 8
    up_steps = [[(2 * z + y, 2 * z + 2 + y) for z in range(k - 1, 3) for y in range(2)] for k in (1, 2, 3)]
    down_steps = [[(2 * z + y, 2 * z - 2 + y) for z in range(1, 5 - k) for y in range(2)] for k in (1, 2, 3)]
    y_pairs = [(i, i ^ 1) for i in range(dp_size)]

    one = jnp.where(dp_place < 0, 0.5, 1.0).astype(wide)

    def rounded(v):
        return (v * one).astype(bfloat)

    def swap_core(v):
        return lax.ppermute(v, "tensor", CORE_PAIRS)

    def swap_x(v):
        return lax.ppermute(v, "tensor", X_PAIRS)

    def my_half(v):
        return lax.dynamic_slice_in_dim(v, core * half, half, 0)

    def other_half(v):
        return lax.dynamic_slice_in_dim(v, (1 - core) * half, half, 0)

    def natural(mine, other):
        return jnp.where(
            core == 0, jnp.concatenate([mine, other], 0), jnp.concatenate([other, mine], 0)
        )

    def total_half(mine, other):
        both = mine + swap_core(other)
        return both + swap_x(both)

    def along_z(v):
        z = dp_place // 2
        ups, downs = [v], [v]
        for k in range(3):
            ups.append(lax.ppermute(ups[-1], "dp", up_steps[k]))
            downs.append(lax.ppermute(downs[-1], "dp", down_steps[k]))
        return [jnp.where(z >= k, ups[k], downs[4 - k]) for k in (1, 2, 3)]

    def sum_blocks(blocks):
        if not small:
            return lax.psum_scatter(blocks, "dp", scatter_dimension=0, tiled=True)[0]
        y, z = dp_place % 2, dp_place // 2
        split = blocks.reshape((4, 2) + blocks.shape[1:])
        kept = lax.dynamic_index_in_dim(split, y, 1, False)
        sent = lax.dynamic_index_in_dim(split, 1 - y, 1, False)
        kept = kept + lax.ppermute(sent, "dp", y_pairs)
        total = lax.dynamic_index_in_dim(kept, z, 0, False)
        for k in (1, 2, 3):
            part = lax.dynamic_index_in_dim(kept, (z + k) % 4, 0, False)
            total = total + lax.ppermute(part, "dp", [(i, (i + 2 * k) % 8) for i in range(8)])
        return total

    out_wide = out_grad.astype(wide)
    lane = jnp.arange(EXPERTS, dtype=jnp.int32)
    dense_gates = jnp.sum(
        jnp.where(routes[:, :, None] == lane[None, None, :], gates[:, :, None], 0.0), 1
    )
    local_order = lambda v: jnp.concatenate([my_half(v), other_half(v)], 0)
    if small:
        og_z = along_z(my_half(out_wide))
        gates_z = along_z(dense_gates.T)

    tokens_wide = tokens.astype(wide)
    normed1_low = norm_forward(tokens_wide, norm1_gain).astype(bfloat)
    query_proj = dot_nn(normed1_low, w_query)
    key_proj = dot_nn(normed1_low, w_key)
    value_low = (
        dot_nn(normed1_low, w_value).astype(bfloat).reshape(row_count, local_groups, HEAD_DIM)
    )
    cosine, sine_table = rope_tables(positions)

    def turn_query(proj_in):
        return rotate(proj_in.reshape(row_count, local_heads, HEAD_DIM), cosine, sine_table)

    def turn_key(proj_in):
        return rotate(proj_in.reshape(row_count, local_groups, HEAD_DIM), cosine, sine_table)

    query_rot, query_back = jax.vjp(turn_query, query_proj)
    key_rot, key_back = jax.vjp(turn_key, key_proj)
    query_low = query_rot.astype(bfloat).reshape(row_count, local_groups, per_group, HEAD_DIM)
    key_low = key_rot.astype(bfloat)
    key_index = jnp.arange(row_count, dtype=jnp.int32)

    def block_scores(block_num):
        row_start = block_num * block_rows
        query_block = query_low[row_start : row_start + block_rows]
        row_index = row_start + jnp.arange(block_rows, dtype=jnp.int32)
        place_gap = positions[row_start : row_start + block_rows][:, None] - positions[None, :]
        allowed = (row_index[:, None] >= key_index[None, :]) & (
            place_gap == row_index[:, None] - key_index[None, :]
        )
        raw_scores = (
            jnp.einsum("qgrd,kgd->grqk", query_block, key_low, preferred_element_type=wide)
            * scale_factor
        )
        return (jnp.where(allowed[None, None], raw_scores, -1e30), query_block)

    mixed_blocks = []
    log_totals = []
    for block_num in range(block_count):
        scores, query_block = block_scores(block_num)
        row_max = jnp.max(scores, -1, keepdims=True)
        exp_scores = jnp.exp(scores - row_max)
        row_total = jnp.sum(exp_scores, -1, keepdims=True)
        soft_low = (exp_scores / row_total).astype(bfloat)
        log_totals.append(row_max + jnp.log(row_total))
        mixed_blocks.append(
            jnp.einsum("grqk,kgd->qgrd", soft_low, value_low, preferred_element_type=wide)
        )
    mixed_low = (
        jnp.concatenate(mixed_blocks, 0).astype(bfloat).reshape(row_count, local_heads * HEAD_DIM)
    )
    attention = total_half(
        dot_nn(my_half(mixed_low), w_out), dot_nn(other_half(mixed_low), w_out)
    )
    hidden = my_half(tokens_wide) + attention
    normed2 = norm_forward(hidden, norm2_gain)
    normed2_mine = normed2.astype(bfloat)
    normed2_other = rounded(swap_core(normed2))
    og_mine, og_other = my_half(out_grad), other_half(out_grad)
    gates_mine, gates_other = my_half(dense_gates), other_half(dense_gates)
    own_other = own_experts(normed2_other, og_other, gates_other, w_gate, w_up, w_down)
    own_mine = own_experts(normed2_mine, og_mine, gates_mine, w_gate, w_up, w_down)

    normed2_grad = total_half(own_mine[3], own_other[3])
    hidden_part, gain2_grad = norm_backward(hidden, norm2_gain, normed2_grad)
    hidden_grad = my_half(out_wide) + hidden_part
    attn_grad = natural(hidden_grad.astype(bfloat), rounded(swap_core(hidden_grad)))

    w_down2 = w_down.reshape(-1, width)
    expert_total = total_half(dot_nn(own_mine[0], w_down2), dot_nn(own_other[0], w_down2))
    block_mine = hidden + expert_total
    block_out = natural(block_mine, swap_core(block_mine))

    if small:
        quarter = half // 2
        normed2_z = along_z(lax.dynamic_slice_in_dim(normed2, x_side * quarter, quarter, 0))
        n2_q = jnp.stack(normed2_z)
        n2_x = swap_x(n2_q)
        n2_h = jnp.where(
            x_side == 0, jnp.concatenate([n2_q, n2_x], 1), jnp.concatenate([n2_x, n2_q], 1)
        )
        n2_o = swap_core(n2_h)
        x_all = rounded(jnp.concatenate([n2_h, n2_o], 1)).reshape(3 * row_count, width)
        og_h = jnp.stack(og_z)
        og_o = swap_core(og_h)
        og_all = rounded(jnp.concatenate([og_h, og_o], 1)).reshape(3 * row_count, width)
        gates_all = jnp.concatenate([local_order(v.T) for v in gates_z], 0)
        shard = width // dp_size

        def two_blocks(other, mine, rest):
            cut = lambda v, place: lax.dynamic_slice_in_dim(v, place * shard, shard, 1)
            return jnp.concatenate(
                [
                    jnp.concatenate([cut(v, place).T for v in (other, mine, rest)], 1)
                    for place in (dp_place, dp_place ^ 1)
                ],
                0,
            )

        xt = two_blocks(x_all, normed2_mine, normed2_other)
        ogt = two_blocks(og_all, og_mine, og_other)
        chunks = []
        for chunk in range(CHUNKS):
            kg, sg, ku, su, kd, sd = expert_grads(
                chunk, x_all, og_all, gates_all, xt, ogt, own_mine[:3], own_other[:3],
                w_gate, w_up, w_down,
            )
            chunks.append(
                [k + lax.ppermute(s, "dp", y_pairs) for k, s in ((kg, sg), (ku, su), (kd, sd))]
            )
        grad_w_gate, grad_w_up, grad_w_down = (
            jnp.concatenate([c[i] for c in chunks], 0) for i in range(3)
        )
    else:
        n2_own = jnp.concatenate([normed2_mine, normed2_other], 0)
        og_own = jnp.concatenate([og_mine, og_other], 0)
        ga, gg, ug = (
            jnp.concatenate([own_mine[i], own_other[i]], 0).reshape(row_count, EXPERTS, -1)
            for i in range(3)
        )
        grad_w_gate = jnp.einsum("td,tef->edf", n2_own, gg, preferred_element_type=wide)
        grad_w_up = jnp.einsum("td,tef->edf", n2_own, ug, preferred_element_type=wide)
        grad_w_down = jnp.einsum("tef,td->efd", ga, og_own, preferred_element_type=wide)
        grad_w_gate = lax.psum_scatter(grad_w_gate, "dp", scatter_dimension=1, tiled=True)
        grad_w_up = lax.psum_scatter(grad_w_up, "dp", scatter_dimension=1, tiled=True)
        grad_w_down = lax.psum_scatter(grad_w_down, "dp", scatter_dimension=2, tiled=True)

    grad_w_out = jnp.einsum("tc,td->cd", mixed_low, attn_grad, preferred_element_type=wide)
    mixed_grad = dot_nt(attn_grad, w_out).astype(bfloat)
    mixed_grad = mixed_grad.reshape(row_count, local_groups, per_group, HEAD_DIM)
    key_grad = jnp.zeros((row_count, local_groups, HEAD_DIM), wide)
    value_grad = jnp.zeros((row_count, local_groups, HEAD_DIM), wide)
    query_grads = []
    for block_num in range(block_count):
        row_start = block_num * block_rows
        scores, query_block = block_scores(block_num)
        soft = jnp.exp(scores - log_totals[block_num])
        grad_block = mixed_grad[row_start : row_start + block_rows]
        prob_grad = jnp.einsum("qgrd,kgd->grqk", grad_block, value_low, preferred_element_type=wide)
        row_dot = jnp.sum(soft * prob_grad, -1, keepdims=True)
        score_grad = (soft * (prob_grad - row_dot)).astype(bfloat)
        query_grads.append(
            jnp.einsum("grqk,kgd->qgrd", score_grad, key_low, preferred_element_type=wide)
            * scale_factor
        )
        key_grad = (
            key_grad
            + jnp.einsum("grqk,qgrd->kgd", score_grad, query_block, preferred_element_type=wide)
            * scale_factor
        )
        value_grad = value_grad + jnp.einsum(
            "grqk,qgrd->kgd", soft.astype(bfloat), grad_block, preferred_element_type=wide
        )
    query_rot_grad = jnp.concatenate(query_grads, 0).reshape(row_count, local_heads, HEAD_DIM)
    (query_in,) = query_back(query_rot_grad)
    (key_in,) = key_back(key_grad)
    qkv_low = jnp.concatenate(
        [
            query_in.astype(bfloat),
            key_in.astype(bfloat),
            value_grad.astype(bfloat).reshape(row_count, local_groups * HEAD_DIM),
        ],
        1,
    )
    w_qkv = jnp.concatenate([w_query, w_key, w_value], 1)
    normed1_grad = total_half(dot_nt(my_half(qkv_low), w_qkv), dot_nt(other_half(qkv_low), w_qkv))
    tokens_mine = my_half(tokens_wide)
    tokens_part, gain1_grad = norm_backward(tokens_mine, norm1_gain, normed1_grad)
    tokens_half = hidden_grad + tokens_part
    tokens_grad = natural(tokens_half, swap_core(tokens_half))

    grad_w_qkv = jnp.einsum("td,tc->dc", normed1_low, qkv_low, preferred_element_type=wide)
    grad_w_qkv = sum_blocks(grad_w_qkv.reshape(dp_size, width // dp_size, -1))
    grad_w_out = sum_blocks(
        grad_w_out.reshape(w_out.shape[0], dp_size, width // dp_size).transpose(1, 0, 2)
    )
    gain1 = sum_blocks((gain1_grad + swap_core(gain1_grad)).reshape(dp_size, -1))
    gain2 = sum_blocks((gain2_grad + swap_core(gain2_grad)).reshape(dp_size, -1))
    query_cols, key_cols = w_query.shape[1], w_key.shape[1]
    return (
        block_out,
        tokens_grad,
        gain1,
        grad_w_qkv[:, :query_cols],
        grad_w_qkv[:, query_cols : query_cols + key_cols],
        grad_w_qkv[:, query_cols + key_cols :],
        grad_w_out,
        gain2,
        grad_w_gate,
        grad_w_up,
        grad_w_down,
    )


def solution(mesh):
    placed = (
        P("dp", None),
        P("dp"),
        P("dp", None),
        P("dp", None),
        P(),
        P(None, "tensor"),
        P(None, "tensor"),
        P(None, "tensor"),
        P("tensor", None),
        P(),
        P(None, None, "tensor"),
        P(None, None, "tensor"),
        P(None, "tensor", None),
        P("dp", None),
    )
    return jax.shard_map(
        functools.partial(per_device, mesh.shape["dp"]),
        mesh=mesh,
        in_specs=placed,
        out_specs=(
            P("dp", None),
            P("dp", None),
            P("dp"),
            P("dp", "tensor"),
            P("dp", "tensor"),
            P("dp", "tensor"),
            P("tensor", "dp"),
            P("dp"),
            P(None, "dp", "tensor"),
            P(None, "dp", "tensor"),
            P(None, "tensor", "dp"),
        ),
        check_vma=False,
    )
```

```python
import functools

import jax
import jax.numpy as jnp
from jax import lax
from jax.experimental import pallas as pl
from jax.experimental.pallas import tpu as pltpu
from jax.sharding import PartitionSpec as P

HEAD_DIM = 64
EXPERTS = 32
TOP = 8
EPS = 1e-06
ROPE_BASE = 10000.0
CHUNK_SIZES = (8, 8, 8, 8)

bfloat = jnp.bfloat16
wide = jnp.float32

BRIEF = pl.CostEstimate(flops=2**20, bytes_accessed=2**20, transcendentals=0)

CORE_PAIRS = [(i, i ^ 1) for i in range(4)]
X_PAIRS = [(i, i ^ 2) for i in range(4)]


def dot_nn(a, b):
    return jnp.dot(a, b, preferred_element_type=wide)


def dot_nt(a, b):
    return lax.dot_general(a, b, (((1,), (1,)), ((), ())), preferred_element_type=wide)


def norm_forward(v, gain):
    return v * lax.rsqrt(jnp.mean(v * v, -1, keepdims=True) + EPS) * gain


def norm_backward(v, gain, q):
    r = lax.rsqrt(jnp.mean(v * v, -1, keepdims=True) + EPS)
    gq = gain * q
    v_grad = r * gq - v * (r * r * r) * jnp.mean(v * gq, -1, keepdims=True)
    return v_grad, jnp.sum(q * v * r, 0)


def rope_tables(positions):
    half_dim = HEAD_DIM // 2
    freqs = ROPE_BASE ** (-(jnp.arange(half_dim, dtype=jnp.float32) * 2.0) / HEAD_DIM)
    angles = positions.astype(jnp.float32)[:, None] * freqs[None, :]
    cosine = jnp.cos(angles)
    sine_table = jnp.sin(angles)
    return (jnp.concatenate([cosine, cosine], -1), jnp.concatenate([sine_table, sine_table], -1))


def rotate(values_in, cosine, sine_table):
    half_dim = values_in.shape[-1] // 2
    turned = jnp.concatenate([-values_in[..., half_dim:], values_in[..., :half_dim]], -1)
    return values_in * cosine[:, None, :] + turned * sine_table[:, None, :]


def expert_parts(x, og, gate_cols, w_pair, wd2):
    hidden = wd2.shape[0] // 2
    back = dot_nt(og, wd2)
    out = []
    for j in range(2):
        both = dot_nn(x, w_pair[j])
        gate, up = both[:, :hidden], both[:, hidden:]
        col = gate_cols[j]
        sig = 0.5 * jnp.tanh(0.5 * gate) + 0.5
        act = gate * sig
        slope = sig + act * (1.0 - sig)
        weighted = back[:, j * hidden : (j + 1) * hidden] * col
        out.append(
            (
                (act * up * col).astype(bfloat),
                (weighted * up * slope).astype(bfloat),
                (weighted * act).astype(bfloat),
            )
        )
    return out


def gate_columns(g, first):
    lane = lax.broadcasted_iota(jnp.int32, g.shape, 1)
    return [
        jnp.sum(jnp.where(lane == first + j, g, 0.0), axis=1, keepdims=True) for j in range(2)
    ]


def own_body(x_ref, og_ref, g_ref, wg_ref, wu_ref, wd_ref, ga_ref, gu_ref, n_ref):
    pair = pl.program_id(0)
    hidden = wg_ref.shape[2]

    @pl.when(pair == 0)
    def _():
        n_ref[...] = jnp.zeros_like(n_ref)

    w_pair = [jnp.concatenate([wg_ref[j], wu_ref[j]], axis=1) for j in range(2)]
    wd2 = wd_ref[...].reshape(2 * hidden, wd_ref.shape[2])
    cols = gate_columns(g_ref[...], 2 * pair)
    parts = expert_parts(x_ref[...], og_ref[...], cols, w_pair, wd2)
    total = n_ref[...]
    for j in range(2):
        ga, gg, ug = parts[j]
        ga_ref[:, j * hidden : (j + 1) * hidden] = ga
        gu = jnp.concatenate([gg, ug], axis=1)
        gu_ref[:, 2 * j * hidden : 2 * (j + 1) * hidden] = gu
        total = total + dot_nt(gu, w_pair[j])
    n_ref[...] = total


def whole(a):
    return pl.BlockSpec(a.shape, lambda *_: (0,) * a.ndim, pipeline_mode=pl.Buffered(1))


def own_experts(x, og, g, w_gate, w_up, w_down):
    rows, width = x.shape
    experts, _, hidden = w_gate.shape
    up_spec = pl.BlockSpec((2, width, hidden), lambda p: (p, 0, 0))
    return pl.pallas_call(
        own_body,
        grid=(experts // 2,),
        in_specs=[
            whole(x),
            whole(og),
            whole(g),
            up_spec,
            up_spec,
            pl.BlockSpec((2, hidden, width), lambda p: (p, 0, 0)),
        ],
        out_specs=[
            pl.BlockSpec((rows, 2 * hidden), lambda p: (0, p)),
            pl.BlockSpec((rows, 4 * hidden), lambda p: (0, p)),
            pl.BlockSpec((rows, width), lambda p: (0, 0)),
        ],
        out_shape=[
            jax.ShapeDtypeStruct((rows, experts * hidden), bfloat),
            jax.ShapeDtypeStruct((rows, 2 * experts * hidden), bfloat),
            jax.ShapeDtypeStruct((rows, width), wide),
        ],
        compiler_params=pltpu.CompilerParams(
            dimension_semantics=("arbitrary",), vmem_limit_bytes=40 * 2**20
        ),
        cost_estimate=BRIEF,
        name="own_experts",
    )(x, og, g, w_gate, w_up, w_down)


def grads_body(first, parts_n, *refs):
    x_refs, og_refs, g_refs, xt_refs, ogt_refs = (
        refs[parts_n * i : parts_n * (i + 1)] for i in range(5)
    )
    own_xt, own_ogt, own_ga, own_gu, wg_ref, wu_ref, wd_ref, keep, send = refs[
        5 * parts_n : 5 * parts_n + 9
    ]
    s_refs, sa_ref = refs[-3:-1], refs[-1]
    pair = pl.program_id(0)
    hidden = wg_ref.shape[2]
    w_pair = [jnp.concatenate([wg_ref[j], wu_ref[j]], axis=1) for j in range(2)]
    wd2 = wd_ref[...].reshape(2 * hidden, wd_ref.shape[2])
    rows = x_refs[0].shape[0]

    for n in range(parts_n):
        to = slice(n * rows, (n + 1) * rows)
        cols = gate_columns(g_refs[n][...], 2 * (pair + first))
        parts = expert_parts(x_refs[n][...], og_refs[n][...], cols, w_pair, wd2)
        for j in range(2):
            ga, gg, ug = parts[j]
            sa_ref[to, j * hidden : (j + 1) * hidden] = ga
            s_refs[j][to, :hidden] = gg
            s_refs[j][to, hidden:] = ug

    def total(transposed, own_transposed, scratch, own):
        out = dot_nn(own_transposed[...], own)
        for n in range(parts_n):
            out = out + dot_nn(transposed[n][...], scratch[n * rows : (n + 1) * rows])
        return out

    shard = own_xt.shape[0] // 2
    for j in range(2):
        lanes = slice(2 * j * hidden, 2 * (j + 1) * hidden)
        grad = total(xt_refs, own_xt, s_refs[j], own_gu[:, lanes])
        for i in range(2):
            keep[j, i] = grad[:shard, i * hidden : (i + 1) * hidden]
            send[j, i] = grad[shard:, i * hidden : (i + 1) * hidden]
    down = total(ogt_refs, own_ogt, sa_ref, own_ga[...])
    for j in range(2):
        turned = down[:, j * hidden : (j + 1) * hidden].T
        keep[j, 2] = turned[:, :shard]
        send[j, 2] = turned[:, shard:]


def expert_grads(first_expert, count, x, og, g, xt, ogt, own_xt, own_ogt, own_ga, own_gu, weights):
    rows, width = x[0].shape
    w_gate, w_up, w_down = weights
    _, _, hidden = w_gate.shape
    own_rows = own_ga.shape[0]
    all_rows = len(x) * rows
    shard = own_xt.shape[0] // 2
    first = first_expert // 2
    up_spec = pl.BlockSpec((2, width, hidden), lambda p: (p + first, 0, 0))
    out_spec = pl.BlockSpec((2, 3, shard, hidden), lambda p: (p, 0, 0, 0))
    out_shape = jax.ShapeDtypeStruct((count, 3, shard, hidden), wide)
    resident = (*x, *og, *g, *xt, *ogt, own_xt, own_ogt)
    return pl.pallas_call(
        functools.partial(grads_body, first, len(x)),
        grid=(count // 2,),
        in_specs=[whole(a) for a in resident]
        + [pl.BlockSpec((own_rows, 2 * hidden), lambda p: (0, p + first))]
        + [pl.BlockSpec((own_rows, 4 * hidden), lambda p: (0, p + first))]
        + [up_spec, up_spec, pl.BlockSpec((2, hidden, width), lambda p: (p + first, 0, 0))],
        out_specs=[out_spec] * 2,
        out_shape=[out_shape] * 2,
        scratch_shapes=[pltpu.VMEM((all_rows, 2 * hidden), bfloat)] * 3,
        compiler_params=pltpu.CompilerParams(
            dimension_semantics=("arbitrary",), vmem_limit_bytes=56 * 2**20
        ),
        cost_estimate=BRIEF,
        name="expert_grads",
    )(*resident, own_ga, own_gu, *weights)


def prepare_body(normed, place_ref, mine_ref, other_ref, gain_ref, x_ref, t_ref):
    shard = t_ref.shape[0] // 2
    blocks = pl.num_programs(0) // 2

    def emit(v_ref):
        v = v_ref[...]
        if normed:
            scale = lax.rsqrt(jnp.mean(v * v, -1, keepdims=True) + EPS)
            v = v * scale * gain_ref[...]
        x_ref[...] = v.astype(bfloat)
        for i in range(2):
            cols = pl.ds(pl.multiple_of((place_ref[0] ^ i) * shard, shard), shard)
            cut = v_ref[:, cols]
            if normed:
                cut = cut * scale * gain_ref[:, cols]
            t_ref[i * shard : (i + 1) * shard, :] = cut.T.astype(bfloat)

    @pl.when(pl.program_id(0) < blocks)
    def _():
        emit(mine_ref)

    @pl.when(pl.program_id(0) >= blocks)
    def _():
        emit(other_ref)


def prepare(mine, other, gain, place, shard, half, normed):
    width = mine.shape[1]
    block = 256
    blocks = half // block
    return pl.pallas_call(
        functools.partial(prepare_body, normed),
        grid_spec=pltpu.PrefetchScalarGridSpec(
            num_scalar_prefetch=1,
            grid=(2 * blocks,),
            in_specs=[
                pl.BlockSpec((block, width), lambda i, _: (jnp.minimum(i, blocks - 1), 0)),
                pl.BlockSpec((block, width), lambda i, _: (jnp.maximum(i - blocks, 0), 0)),
                pl.BlockSpec((1, width), lambda i, _: (0, 0)),
            ],
            out_specs=[
                pl.BlockSpec((block, width), lambda i, _: (i, 0)),
                pl.BlockSpec((2 * shard, block), lambda i, _: (0, i)),
            ],
        ),
        out_shape=[
            jax.ShapeDtypeStruct((2 * half, width), bfloat),
            jax.ShapeDtypeStruct((2 * shard, 2 * half), bfloat),
        ],
        cost_estimate=BRIEF,
        name="prepare",
    )(place.reshape(1), mine, other, gain.reshape(1, width))


def place_halves_body(core_ref, mine_ref, other_ref, out_ref):
    half = pl.program_id(0)

    @pl.when(half == 0)
    def _():
        out_ref[...] = mine_ref[...]

    @pl.when(half == 1)
    def _():
        out_ref[...] = other_ref[...]


def place_halves(mine, other, core):
    rows, width = mine.shape
    steps = 2
    block = (rows // steps, width)
    return pl.pallas_call(
        place_halves_body,
        grid_spec=pltpu.PrefetchScalarGridSpec(
            num_scalar_prefetch=1,
            grid=(2, steps),
            in_specs=[
                pl.BlockSpec(block, lambda h, i, _: (jnp.where(h == 0, i, steps - 1), 0)),
                pl.BlockSpec(block, lambda h, i, _: (jnp.where(h == 0, 0, i), 0)),
            ],
            out_specs=pl.BlockSpec(block, lambda h, i, c: ((h ^ c[0]) * steps + i, 0)),
        ),
        out_shape=jax.ShapeDtypeStruct((2 * rows, width), mine.dtype),
        cost_estimate=BRIEF,
        name="place_halves",
    )(core.reshape(1), mine, other)


def after(v, *others):
    return lax.optimization_barrier((v, *others))[0]


def together(*values):
    return lax.optimization_barrier(values)


def per_device(
    dp_size,
    tokens,
    positions,
    routes,
    gates,
    norm1_gain,
    w_query,
    w_key,
    w_value,
    w_out,
    norm2_gain,
    w_gate,
    w_up,
    w_down,
    out_grad,
):
    row_count, width = tokens.shape
    half = row_count // 2
    local_heads = w_query.shape[1] // HEAD_DIM
    local_groups = w_key.shape[1] // HEAD_DIM
    per_group = local_heads // local_groups
    scale_factor = HEAD_DIM ** (-0.5)
    block_rows = min(512, row_count)
    block_count = row_count // block_rows
    core = lax.axis_index("tensor") % 2
    x_side = lax.axis_index("tensor") // 2
    dp_place = lax.axis_index("dp")
    small = dp_size == 8
    z_shifts = {k: [(i, (i + 2 * k) % 8) for i in range(8)] for k in (1, 2, 3)}
    y_pairs = [(i, i ^ 1) for i in range(dp_size)]

    one = jnp.where(dp_place < 0, 0.5, 1.0).astype(wide)

    def rounded(v):
        return (v * one).astype(bfloat)

    def swap_core(v):
        return lax.ppermute(v, "tensor", CORE_PAIRS)

    def swap_x(v):
        return lax.ppermute(v, "tensor", X_PAIRS)

    def my_half(v):
        return lax.dynamic_slice_in_dim(v, core * half, half, 0)

    def other_half(v):
        return lax.dynamic_slice_in_dim(v, (1 - core) * half, half, 0)

    def natural(mine, other):
        return jnp.where(
            core == 0, jnp.concatenate([mine, other], 0), jnp.concatenate([other, mine], 0)
        )

    def total_half(mine, other):
        both = mine + swap_core(other)
        return both + swap_x(both)

    def along_z(v, k):
        return lax.ppermute(v, "dp", z_shifts[k])

    def join_x(mine, other):
        return jnp.where(
            x_side == 0, jnp.concatenate([mine, other], 0), jnp.concatenate([other, mine], 0)
        )

    def sum_z(blocks):
        z = dp_place // 2
        split = blocks.reshape((4, 2) + blocks.shape[1:])
        total = lax.dynamic_index_in_dim(split, z, 0, False)
        for k in (1, 2, 3):
            total = total + along_z(lax.dynamic_index_in_dim(split, (z + k) % 4, 0, False), k)
        return total

    def sum_y(blocks):
        y = dp_place % 2
        kept = lax.dynamic_index_in_dim(blocks, y, 0, False)
        return kept + lax.ppermute(
            lax.dynamic_index_in_dim(blocks, 1 - y, 0, False), "dp", y_pairs
        )

    out_wide = out_grad.astype(wide)
    lane = jnp.arange(EXPERTS, dtype=jnp.int32)
    dense_gates = jnp.sum(
        jnp.where(routes[:, :, None] == lane[None, None, :], gates[:, :, None], 0.0), 1
    )
    quarter = half // 2
    og_mine, og_other = my_half(out_wide), other_half(out_wide)
    gates_mine, gates_other = my_half(dense_gates), other_half(dense_gates)
    shard = width // dp_size

    def my_quarter(v):
        return lax.dynamic_slice_in_dim(v, x_side * quarter, quarter, 0)

    if small:
        og_sent = jnp.concatenate(
            [my_quarter(og_mine), my_quarter(gates_mine).reshape(-1, width)], 0
        )
        og_z = {k: along_z(og_sent, k) for k in (1, 3, 2)}

    tokens_wide = tokens.astype(wide)
    normed1_low = norm_forward(tokens_wide, norm1_gain).astype(bfloat)
    query_proj = dot_nn(normed1_low, w_query)
    key_proj = dot_nn(normed1_low, w_key)
    value_low = (
        dot_nn(normed1_low, w_value).astype(bfloat).reshape(row_count, local_groups, HEAD_DIM)
    )
    cosine, sine_table = rope_tables(positions)

    def turn_query(proj_in):
        return rotate(proj_in.reshape(row_count, local_heads, HEAD_DIM), cosine, sine_table)

    def turn_key(proj_in):
        return rotate(proj_in.reshape(row_count, local_groups, HEAD_DIM), cosine, sine_table)

    query_rot, query_back = jax.vjp(turn_query, query_proj)
    key_rot, key_back = jax.vjp(turn_key, key_proj)
    query_low = query_rot.astype(bfloat).reshape(row_count, local_groups, per_group, HEAD_DIM)
    key_low = key_rot.astype(bfloat)
    key_index = jnp.arange(row_count, dtype=jnp.int32)

    def block_scores(block_num):
        row_start = block_num * block_rows
        query_block = query_low[row_start : row_start + block_rows]
        row_index = row_start + jnp.arange(block_rows, dtype=jnp.int32)
        place_gap = positions[row_start : row_start + block_rows][:, None] - positions[None, :]
        allowed = (row_index[:, None] >= key_index[None, :]) & (
            place_gap == row_index[:, None] - key_index[None, :]
        )
        raw_scores = (
            jnp.einsum("qgrd,kgd->grqk", query_block, key_low, preferred_element_type=wide)
            * scale_factor
        )
        return (jnp.where(allowed[None, None], raw_scores, -1e30), query_block)

    mixed_blocks = []
    log_totals = []
    for block_num in range(block_count):
        scores, query_block = block_scores(block_num)
        row_max = jnp.max(scores, -1, keepdims=True)
        exp_scores = jnp.exp(scores - row_max)
        row_total = jnp.sum(exp_scores, -1, keepdims=True)
        soft_low = (exp_scores / row_total).astype(bfloat)
        log_totals.append(row_max + jnp.log(row_total))
        mixed_blocks.append(
            jnp.einsum("grqk,kgd->qgrd", soft_low, value_low, preferred_element_type=wide)
        )
    mixed_low = (
        jnp.concatenate(mixed_blocks, 0).astype(bfloat).reshape(row_count, local_heads * HEAD_DIM)
    )
    ready = functools.partial(
        prepare,
        gain=norm2_gain,
        place=dp_place if small else jnp.zeros_like(dp_place),
        shard=shard if small else width // 8,
        half=half,
    )
    own_og, own_ogt = ready(og_mine, og_other, normed=False)
    own_gates = jnp.concatenate([gates_mine, gates_other], 0)
    if small:
        mixed_low, og_z[1] = together(mixed_low, og_z[1])
    attn_both = dot_nn(my_half(mixed_low), w_out) + swap_core(
        dot_nn(other_half(mixed_low), w_out)
    )
    attention = after(attn_both + swap_x(attn_both), own_og, own_ogt, own_gates)
    if small:
        attention, og_z[2] = together(attention, og_z[2])
    hidden = my_half(tokens_wide) + attention
    hidden_other = swap_core(hidden)
    weights = (w_gate, w_up, w_down)
    own_x, own_xt = ready(hidden, hidden_other, normed=True)
    ga, gu, n_part = own_experts(own_x, own_og, own_gates, *weights)
    if small:
        z_hidden = {2: along_z(my_quarter(hidden), 2)}
        og_x = {k: swap_x(og_z[k]) for k in (1, 2)}
        n_part, z_hidden[2], og_z[3], og_x[1], og_x[2] = together(
            n_part, z_hidden[2], og_z[3], og_x[1], og_x[2]
        )

    n_both = n_part[:half] + swap_core(n_part[half:])
    normed2_grad = n_both + swap_x(n_both)
    w_down2 = w_down.reshape(-1, width)
    e_both = dot_nn(ga[:half], w_down2) + swap_core(dot_nn(ga[half:], w_down2))
    waiting = [e_both]
    if small:
        def og_part(k):
            og_h = join_x(og_z[k][:quarter], og_x[k][:quarter])
            gates_h = join_x(og_z[k][quarter:], og_x[k][quarter:])
            og_h = jnp.concatenate([og_h, gates_h], 0)
            arrived = swap_core(og_h)
            prepared = ready(og_h, arrived, normed=False)
            both_gates = jnp.concatenate([gates_h, arrived[half:]], 0).reshape(-1, EXPERTS)
            return (*prepared, both_gates)

        og_parts = {k: og_part(k) for k in (1, 2)}
        z_hidden[1] = along_z(after(hidden, n_part), 1)
        waiting += [z_hidden[1], *og_parts[1], *og_parts[2]]
    normed2_grad, e_both, *waited = together(normed2_grad, *waiting)
    if small:
        z_hidden[1] = waited[0]
        og_parts = {1: waited[1:4], 2: waited[4:7]}
    hidden_part, gain2_grad = norm_backward(hidden, norm2_gain, normed2_grad)
    hidden_grad = my_half(out_wide) + hidden_part
    attn_grad = natural(hidden_grad.astype(bfloat), rounded(swap_core(hidden_grad)))
    if small:
        z_hidden[3] = along_z(after(hidden, normed2_grad), 3)
        og_x[3] = swap_x(after(og_z[3], normed2_grad))
        hidden_x = swap_x(after(z_hidden[2], normed2_grad))

    grad_w_out = jnp.einsum("tc,td->cd", mixed_low, attn_grad, preferred_element_type=wide)
    mixed_grad = dot_nt(attn_grad, w_out).astype(bfloat)
    mixed_grad = mixed_grad.reshape(row_count, local_groups, per_group, HEAD_DIM)
    key_grad = jnp.zeros((row_count, local_groups, HEAD_DIM), wide)
    value_grad = jnp.zeros((row_count, local_groups, HEAD_DIM), wide)
    query_grads = []
    for block_num in range(block_count):
        row_start = block_num * block_rows
        scores, query_block = block_scores(block_num)
        soft = jnp.exp(scores - log_totals[block_num])
        grad_block = mixed_grad[row_start : row_start + block_rows]
        prob_grad = jnp.einsum("qgrd,kgd->grqk", grad_block, value_low, preferred_element_type=wide)
        row_dot = jnp.sum(soft * prob_grad, -1, keepdims=True)
        score_grad = (soft * (prob_grad - row_dot)).astype(bfloat)
        query_grads.append(
            jnp.einsum("grqk,kgd->qgrd", score_grad, key_low, preferred_element_type=wide)
            * scale_factor
        )
        key_grad = (
            key_grad
            + jnp.einsum("grqk,qgrd->kgd", score_grad, query_block, preferred_element_type=wide)
            * scale_factor
        )
        value_grad = value_grad + jnp.einsum(
            "grqk,qgrd->kgd", soft.astype(bfloat), grad_block, preferred_element_type=wide
        )
    query_rot_grad = jnp.concatenate(query_grads, 0).reshape(row_count, local_heads, HEAD_DIM)
    (query_in,) = query_back(query_rot_grad)
    (key_in,) = key_back(key_grad)
    qkv_low = jnp.concatenate(
        [
            query_in.astype(bfloat),
            key_in.astype(bfloat),
            value_grad.astype(bfloat).reshape(row_count, local_groups * HEAD_DIM),
        ],
        1,
    )
    w_qkv = jnp.concatenate([w_query, w_key, w_value], 1)
    if small:
        qkv_low, og_x[3], hidden_x, z_hidden[3] = together(
            qkv_low, og_x[3], hidden_x, z_hidden[3]
        )
    t_both = dot_nt(my_half(qkv_low), w_qkv) + swap_core(dot_nt(other_half(qkv_low), w_qkv))
    normed1_grad = t_both + swap_x(t_both)
    tokens_mine = my_half(tokens_wide)
    tokens_part, gain1_grad = norm_backward(tokens_mine, norm1_gain, normed1_grad)
    tokens_half = hidden_grad + tokens_part
    expert_total = e_both + swap_x(after(e_both, t_both))
    block_mine = hidden + expert_total

    grad_w_qkv = jnp.einsum("td,tc->dc", normed1_low, qkv_low, preferred_element_type=wide)
    gain2_grad = gain2_grad + swap_core(gain2_grad)
    joined = jnp.concatenate(
        [
            grad_w_qkv.reshape(dp_size, grad_w_qkv.shape[1], shard),
            grad_w_out.reshape(w_out.shape[0], dp_size, shard).transpose(1, 0, 2),
            jnp.broadcast_to(gain2_grad.reshape(dp_size, 1, shard), (dp_size, 8, shard)),
        ],
        1,
    )
    gain1_grad = (gain1_grad + swap_core(gain1_grad)).reshape(dp_size, -1)

    if small:
        og_parts[3] = og_part(3)
        hidden_parts = {}
        for k in (1, 2, 3):
            hidden_h = z_hidden[k] if k != 2 else join_x(z_hidden[2], hidden_x)
            hidden_parts[k] = ready(hidden_h, swap_core(hidden_h), normed=True)
        shifts = (1, 2, 3)
        xs = [hidden_parts[k][0] for k in shifts]
        xs = list(lax.optimization_barrier((*xs, t_both))[:3])
        pieces = []
        first = 0
        joined = sum_z(joined)
        for number, count in enumerate(CHUNK_SIZES):
            if number == 1:
                *xs, tokens_half, joined = together(*xs, tokens_half, joined)
                joined = sum_y(joined)
                gain1 = sum_z(gain1_grad)
            if number == 2:
                *xs, block_mine, gain1, pieces[0] = together(*xs, block_mine, gain1, pieces[0])
                gain1 = sum_y(gain1)
            if number == 3:
                *xs, joined, gain1, pieces[1] = together(*xs, joined, gain1, pieces[1])
            keep, send = expert_grads(
                first,
                count,
                xs,
                [og_parts[k][0] for k in shifts],
                [og_parts[k][2] for k in shifts],
                [hidden_parts[k][1] for k in shifts],
                [og_parts[k][1] for k in shifts],
                own_xt,
                own_ogt,
                ga,
                gu,
                weights,
            )
            first += count
            pieces.append(keep + lax.ppermute(send, "dp", y_pairs))
        block_out = place_halves(block_mine, swap_core(block_mine), core)
        tokens_grad = place_halves(tokens_half, swap_core(tokens_half), core)
        *pieces, block_out, tokens_grad = together(*pieces, block_out, tokens_grad)
        grad_w_gate, grad_w_up, grad_w_down = (
            jnp.concatenate([c[:, i] for c in pieces], 0) for i in range(3)
        )
    else:
        joined = lax.psum_scatter(joined, "dp", scatter_dimension=0, tiled=True)[0]
        gain1 = lax.psum_scatter(gain1_grad, "dp", scatter_dimension=0, tiled=True)[0]
        block_out = place_halves(block_mine, swap_core(block_mine), core)
        tokens_grad = place_halves(tokens_half, swap_core(tokens_half), core)
        ga = ga.reshape(row_count, EXPERTS, -1)
        gu = gu.reshape(row_count, EXPERTS, 2, -1)
        grad_w_gate = jnp.einsum("td,tef->edf", own_x, gu[:, :, 0], preferred_element_type=wide)
        grad_w_up = jnp.einsum("td,tef->edf", own_x, gu[:, :, 1], preferred_element_type=wide)
        grad_w_down = jnp.einsum("tef,td->efd", ga, own_og, preferred_element_type=wide)
        grad_w_gate = lax.psum_scatter(grad_w_gate, "dp", scatter_dimension=1, tiled=True)
        grad_w_up = lax.psum_scatter(grad_w_up, "dp", scatter_dimension=1, tiled=True)
        grad_w_down = lax.psum_scatter(grad_w_down, "dp", scatter_dimension=2, tiled=True)

    qkv_rows = grad_w_qkv.shape[1]
    grad_w_qkv = joined[:qkv_rows].reshape(shard, -1)
    grad_w_out = joined[qkv_rows : qkv_rows + w_out.shape[0]]
    gain2 = joined[-8]
    query_cols, key_cols = w_query.shape[1], w_key.shape[1]
    return (
        block_out,
        tokens_grad,
        gain1,
        grad_w_qkv[:, :query_cols],
        grad_w_qkv[:, query_cols : query_cols + key_cols],
        grad_w_qkv[:, query_cols + key_cols :],
        grad_w_out,
        gain2,
        grad_w_gate,
        grad_w_up,
        grad_w_down,
    )


def solution(mesh):
    placed = (
        P("dp", None),
        P("dp"),
        P("dp", None),
        P("dp", None),
        P(),
        P(None, "tensor"),
        P(None, "tensor"),
        P(None, "tensor"),
        P("tensor", None),
        P(),
        P(None, None, "tensor"),
        P(None, None, "tensor"),
        P(None, "tensor", None),
        P("dp", None),
    )
    return jax.shard_map(
        functools.partial(per_device, mesh.shape["dp"]),
        mesh=mesh,
        in_specs=placed,
        out_specs=(
            P("dp", None),
            P("dp", None),
            P("dp"),
            P("dp", "tensor"),
            P("dp", "tensor"),
            P("dp", "tensor"),
            P("tensor", "dp"),
            P("dp"),
            P(None, "dp", "tensor"),
            P(None, "dp", "tensor"),
            P(None, "tensor", "dp"),
        ),
        check_vma=False,
    )
```

```python
import functools

import jax
import jax.numpy as jnp
from jax import lax
from jax.experimental import pallas as pl
from jax.experimental.pallas import tpu as pltpu
from jax.sharding import PartitionSpec as P

HEAD_DIM = 64
EXPERTS = 32
TOP = 8
EPS = 1e-06
ROPE_BASE = 10000.0
CHUNK_SIZES = (8, 10, 8, 6)

bfloat = jnp.bfloat16
wide = jnp.float32

BRIEF = pl.CostEstimate(flops=2**20, bytes_accessed=2**20, transcendentals=0)

CORE_PAIRS = [(i, i ^ 1) for i in range(4)]
X_PAIRS = [(i, i ^ 2) for i in range(4)]


def dot_nn(a, b):
    return jnp.dot(a, b, preferred_element_type=wide)


def dot_nt(a, b):
    return lax.dot_general(a, b, (((1,), (1,)), ((), ())), preferred_element_type=wide)


def norm_forward(v, gain):
    return v * lax.rsqrt(jnp.mean(v * v, -1, keepdims=True) + EPS) * gain


def norm_backward(v, gain, q):
    r = lax.rsqrt(jnp.mean(v * v, -1, keepdims=True) + EPS)
    gq = gain * q
    v_grad = r * gq - v * (r * r * r) * jnp.mean(v * gq, -1, keepdims=True)
    return v_grad, jnp.sum(q * v * r, 0)


def rope_tables(positions):
    half_dim = HEAD_DIM // 2
    freqs = ROPE_BASE ** (-(jnp.arange(half_dim, dtype=jnp.float32) * 2.0) / HEAD_DIM)
    angles = positions.astype(jnp.float32)[:, None] * freqs[None, :]
    cosine = jnp.cos(angles)
    sine_table = jnp.sin(angles)
    return (jnp.concatenate([cosine, cosine], -1), jnp.concatenate([sine_table, sine_table], -1))


def rotate(values_in, cosine, sine_table):
    half_dim = values_in.shape[-1] // 2
    turned = jnp.concatenate([-values_in[..., half_dim:], values_in[..., :half_dim]], -1)
    return values_in * cosine[:, None, :] + turned * sine_table[:, None, :]


def expert_parts(x, back, gate_cols, w_pair):
    hidden = back.shape[1] // 2
    out = []
    for j in range(2):
        both = dot_nn(x, w_pair[j])
        gate, up = both[:, :hidden], both[:, hidden:]
        col = gate_cols[j]
        sig = 0.5 * jnp.tanh(0.5 * gate) + 0.5
        act = gate * sig
        slope = sig + act * (1.0 - sig)
        weighted = back[:, j * hidden : (j + 1) * hidden].astype(wide) * col
        out.append(
            (
                (act * up * col).astype(bfloat),
                (weighted * up * slope).astype(bfloat),
                (weighted * act).astype(bfloat),
            )
        )
    return out


def gate_columns(g, first):
    lane = lax.broadcasted_iota(jnp.int32, g.shape, 1)
    return [
        jnp.sum(jnp.where(lane == first + j, g, 0.0), axis=1, keepdims=True) for j in range(2)
    ]


def own_body(x_ref, back_ref, g_ref, wg_ref, wu_ref, ga_ref, gu_ref, *n_refs):
    pair = pl.program_id(0)
    hidden = wg_ref.shape[2]

    @pl.when(pair == 0)
    def _():
        for n_ref in n_refs:
            n_ref[...] = jnp.zeros_like(n_ref)

    w_pair = [jnp.concatenate([wg_ref[j], wu_ref[j]], axis=1) for j in range(2)]
    cols = gate_columns(g_ref[...], 2 * pair)
    parts = expert_parts(x_ref[...], back_ref[...], cols, w_pair)
    half = n_refs[0].shape[0]
    totals = [n_ref[...] for n_ref in n_refs]
    for j in range(2):
        ga, gg, ug = parts[j]
        ga_ref[:, j * hidden : (j + 1) * hidden] = ga
        gu = jnp.concatenate([gg, ug], axis=1)
        gu_ref[:, 2 * j * hidden : 2 * (j + 1) * hidden] = gu
        for i in range(2):
            totals[i] = totals[i] + dot_nt(gu[i * half : (i + 1) * half], w_pair[j])
    for n_ref, total in zip(n_refs, totals):
        n_ref[...] = total


def back_body(og_ref, wd_ref, out_ref):
    for i in range(out_ref.shape[0]):
        wd2 = wd_ref[2 * i : 2 * i + 2].reshape(-1, wd_ref.shape[2])
        out_ref[i] = dot_nt(og_ref[...], wd2).astype(bfloat)


def back_through_down(og, w_down):
    rows, width = og.shape
    experts, hidden, _ = w_down.shape
    return pl.pallas_call(
        back_body,
        grid=(experts // 4,),
        in_specs=[whole(og), pl.BlockSpec((4, hidden, width), lambda p: (p, 0, 0))],
        out_specs=pl.BlockSpec((2, rows, 2 * hidden), lambda p: (p, 0, 0)),
        out_shape=jax.ShapeDtypeStruct((experts // 2, rows, 2 * hidden), bfloat),
        compiler_params=pltpu.CompilerParams(
            dimension_semantics=("arbitrary",), vmem_limit_bytes=58 * 2**20
        ),
        cost_estimate=BRIEF,
        name="back_through_down",
    )(og, w_down)


def down_body(ga_ref, wd_ref, *out_refs):
    @pl.when(pl.program_id(0) == 0)
    def _():
        for out_ref in out_refs:
            out_ref[...] = jnp.zeros_like(out_ref)

    wd = wd_ref[...].reshape(-1, wd_ref.shape[2])
    half = out_refs[0].shape[0]
    for i, out_ref in enumerate(out_refs):
        rows = slice(i * half, (i + 1) * half)
        ga = jnp.concatenate([ga_ref[n, rows, :] for n in range(ga_ref.shape[0])], axis=1)
        out_ref[...] += dot_nn(ga, wd)


def down_products(ga, w_down):
    rows = ga.shape[1]
    experts, hidden, width = w_down.shape
    out = jax.ShapeDtypeStruct((rows // 2, width), wide)
    return pl.pallas_call(
        down_body,
        grid=(experts // 4,),
        in_specs=[
            pl.BlockSpec((2, rows, 2 * hidden), lambda p: (p, 0, 0)),
            pl.BlockSpec((4, hidden, width), lambda p: (p, 0, 0)),
        ],
        out_specs=[pl.BlockSpec((rows // 2, width), lambda p: (0, 0))] * 2,
        out_shape=[out, out],
        compiler_params=pltpu.CompilerParams(
            dimension_semantics=("arbitrary",), vmem_limit_bytes=58 * 2**20
        ),
        cost_estimate=BRIEF,
        name="down_products",
    )(ga, w_down)


def whole(a):
    return pl.BlockSpec(a.shape, lambda *_: (0,) * a.ndim, pipeline_mode=pl.Buffered(1))


def own_experts(x, back, g, w_gate, w_up):
    rows, width = x.shape
    experts, _, hidden = w_gate.shape
    up_spec = pl.BlockSpec((2, width, hidden), lambda p: (p, 0, 0))
    return pl.pallas_call(
        own_body,
        grid=(experts // 2,),
        in_specs=[
            whole(x),
            pl.BlockSpec((None, rows, 2 * hidden), lambda p: (p, 0, 0)),
            whole(g),
            up_spec,
            up_spec,
        ],
        out_specs=[
            pl.BlockSpec((None, rows, 2 * hidden), lambda p: (p, 0, 0)),
            pl.BlockSpec((None, rows, 4 * hidden), lambda p: (p, 0, 0)),
            pl.BlockSpec((rows // 2, width), lambda p: (0, 0)),
            pl.BlockSpec((rows // 2, width), lambda p: (0, 0)),
        ],
        out_shape=[
            jax.ShapeDtypeStruct((experts // 2, rows, 2 * hidden), bfloat),
            jax.ShapeDtypeStruct((experts // 2, rows, 4 * hidden), bfloat),
            jax.ShapeDtypeStruct((rows // 2, width), wide),
            jax.ShapeDtypeStruct((rows // 2, width), wide),
        ],
        compiler_params=pltpu.CompilerParams(
            dimension_semantics=("arbitrary",), vmem_limit_bytes=40 * 2**20
        ),
        cost_estimate=BRIEF,
        name="own_experts",
    )(x, back, g, w_gate, w_up)


def grads_body(first, parts_n, *refs):
    x_refs, g_refs, xt_refs, ogt_refs, back_refs = (
        refs[parts_n * i : parts_n * (i + 1)] for i in range(5)
    )
    own_xt, own_ogt, own_ga, own_gu, wg_ref, wu_ref, keep, send = refs[
        5 * parts_n : 5 * parts_n + 8
    ]
    s_refs, sa_ref = refs[-3:-1], refs[-1]
    pair = pl.program_id(0)
    hidden = wg_ref.shape[2]
    w_pair = [jnp.concatenate([wg_ref[j], wu_ref[j]], axis=1) for j in range(2)]
    rows = x_refs[0].shape[0]

    for n in range(parts_n):
        to = slice(n * rows, (n + 1) * rows)
        cols = gate_columns(g_refs[n][...], 2 * (pair + first))
        parts = expert_parts(x_refs[n][...], back_refs[n][...], cols, w_pair)
        for j in range(2):
            ga, gg, ug = parts[j]
            sa_ref[to, j * hidden : (j + 1) * hidden] = ga
            s_refs[j][to, :hidden] = gg
            s_refs[j][to, hidden:] = ug

    def total(transposed, own_transposed, scratch, own):
        out = dot_nn(own_transposed[...], own)
        for n in range(parts_n):
            out = out + dot_nn(transposed[n][...], scratch[n * rows : (n + 1) * rows])
        return out

    shard = own_xt.shape[0] // 2
    for j in range(2):
        lanes = slice(2 * j * hidden, 2 * (j + 1) * hidden)
        grad = total(xt_refs, own_xt, s_refs[j], own_gu[:, lanes])
        for i in range(2):
            keep[i, j] = grad[:shard, i * hidden : (i + 1) * hidden]
            send[i, j] = grad[shard:, i * hidden : (i + 1) * hidden]
    down = total(ogt_refs, own_ogt, sa_ref, own_ga[...])
    for j in range(2):
        turned = down[:, j * hidden : (j + 1) * hidden].T
        keep[2, j] = turned[:, :shard]
        send[2, j] = turned[:, shard:]


def expert_grads(first_expert, count, x, g, xt, ogt, back, own_xt, own_ogt, own_ga, own_gu, weights):
    rows, width = x[0].shape
    w_gate, w_up = weights
    _, _, hidden = w_gate.shape
    own_rows = own_ga.shape[1]
    all_rows = len(x) * rows
    shard = own_xt.shape[0] // 2
    first = first_expert // 2
    up_spec = pl.BlockSpec((2, width, hidden), lambda p: (p + first, 0, 0))
    out_spec = pl.BlockSpec((3, 2, shard, hidden), lambda p: (0, p, 0, 0))
    out_shape = jax.ShapeDtypeStruct((3, count, shard, hidden), wide)
    resident = (*x, *g, *xt, *ogt)
    pair_spec = lambda n: pl.BlockSpec((None, n, 2 * hidden), lambda p: (p + first, 0, 0))
    return pl.pallas_call(
        functools.partial(grads_body, first, len(x)),
        grid=(count // 2,),
        in_specs=[whole(a) for a in resident]
        + [pair_spec(rows)] * len(back)
        + [whole(own_xt), whole(own_ogt), pair_spec(own_rows)]
        + [pl.BlockSpec((None, own_rows, 4 * hidden), lambda p: (p + first, 0, 0))]
        + [up_spec, up_spec],
        out_specs=[out_spec] * 2,
        out_shape=[out_shape] * 2,
        scratch_shapes=[pltpu.VMEM((all_rows, 2 * hidden), bfloat)] * 3,
        compiler_params=pltpu.CompilerParams(
            dimension_semantics=("arbitrary",), vmem_limit_bytes=48 * 2**20
        ),
        cost_estimate=pl.CostEstimate(
            flops=count * 2**32, bytes_accessed=count * 2**22, transcendentals=0
        ),
        name="expert_grads",
    )(*resident, *back, own_xt, own_ogt, own_ga, own_gu, *weights)


def prepare_body(normed, place_ref, mine_ref, other_ref, gain_ref, x_ref, t_ref):
    shard = t_ref.shape[0] // 2
    blocks = pl.num_programs(0) // 2

    def emit(v_ref):
        v = v_ref[...]
        if normed:
            scale = lax.rsqrt(jnp.mean(v * v, -1, keepdims=True) + EPS)
            v = v * scale * gain_ref[...]
        x_ref[...] = v.astype(bfloat)
        for i in range(2):
            cols = pl.ds(pl.multiple_of((place_ref[0] ^ i) * shard, shard), shard)
            cut = v_ref[:, cols]
            if normed:
                cut = cut * scale * gain_ref[:, cols]
            t_ref[i * shard : (i + 1) * shard, :] = cut.T.astype(bfloat)

    @pl.when(pl.program_id(0) < blocks)
    def _():
        emit(mine_ref)

    @pl.when(pl.program_id(0) >= blocks)
    def _():
        emit(other_ref)


def prepare(mine, other, gain, place, shard, half, normed):
    width = mine.shape[1]
    block = 256
    blocks = half // block
    return pl.pallas_call(
        functools.partial(prepare_body, normed),
        grid_spec=pltpu.PrefetchScalarGridSpec(
            num_scalar_prefetch=1,
            grid=(2 * blocks,),
            in_specs=[
                pl.BlockSpec((block, width), lambda i, _: (jnp.minimum(i, blocks - 1), 0)),
                pl.BlockSpec((block, width), lambda i, _: (jnp.maximum(i - blocks, 0), 0)),
                pl.BlockSpec((1, width), lambda i, _: (0, 0)),
            ],
            out_specs=[
                pl.BlockSpec((block, width), lambda i, _: (i, 0)),
                pl.BlockSpec((2 * shard, block), lambda i, _: (0, i)),
            ],
        ),
        out_shape=[
            jax.ShapeDtypeStruct((2 * half, width), bfloat),
            jax.ShapeDtypeStruct((2 * shard, 2 * half), bfloat),
        ],
        cost_estimate=BRIEF,
        name="prepare",
    )(place.reshape(1), mine, other, gain.reshape(1, width))


def place_halves_body(core_ref, mine_ref, other_ref, out_ref):
    half = pl.program_id(0)

    @pl.when(half == 0)
    def _():
        out_ref[...] = mine_ref[...]

    @pl.when(half == 1)
    def _():
        out_ref[...] = other_ref[...]


def place_halves(mine, other, core):
    rows, width = mine.shape
    steps = 2
    block = (rows // steps, width)
    return pl.pallas_call(
        place_halves_body,
        grid_spec=pltpu.PrefetchScalarGridSpec(
            num_scalar_prefetch=1,
            grid=(2, steps),
            in_specs=[
                pl.BlockSpec(block, lambda h, i, _: (jnp.where(h == 0, i, steps - 1), 0)),
                pl.BlockSpec(block, lambda h, i, _: (jnp.where(h == 0, 0, i), 0)),
            ],
            out_specs=pl.BlockSpec(block, lambda h, i, c: ((h ^ c[0]) * steps + i, 0)),
        ),
        out_shape=jax.ShapeDtypeStruct((2 * rows, width), mine.dtype),
        cost_estimate=BRIEF,
        name="place_halves",
    )(core.reshape(1), mine, other)


def after(v, *others):
    return lax.optimization_barrier((v, *others))[0]


def together(*values):
    return lax.optimization_barrier(values)


def per_device(
    dp_size,
    tokens,
    positions,
    routes,
    gates,
    norm1_gain,
    w_query,
    w_key,
    w_value,
    w_out,
    norm2_gain,
    w_gate,
    w_up,
    w_down,
    out_grad,
):
    row_count, width = tokens.shape
    half = row_count // 2
    local_heads = w_query.shape[1] // HEAD_DIM
    local_groups = w_key.shape[1] // HEAD_DIM
    per_group = local_heads // local_groups
    scale_factor = HEAD_DIM ** (-0.5)
    block_rows = min(512, row_count)
    block_count = row_count // block_rows
    core = lax.axis_index("tensor") % 2
    x_side = lax.axis_index("tensor") // 2
    dp_place = lax.axis_index("dp")
    small = dp_size == 8
    z_shifts = {k: [(i, (i + 2 * k) % 8) for i in range(8)] for k in (1, 2, 3)}
    y_pairs = [(i, i ^ 1) for i in range(dp_size)]

    one = jnp.where(dp_place < 0, 0.5, 1.0).astype(wide)

    def rounded(v):
        return (v * one).astype(bfloat)

    def swap_core(v):
        return lax.ppermute(v, "tensor", CORE_PAIRS)

    def swap_x(v):
        return lax.ppermute(v, "tensor", X_PAIRS)

    def my_half(v):
        return lax.dynamic_slice_in_dim(v, core * half, half, 0)

    def other_half(v):
        return lax.dynamic_slice_in_dim(v, (1 - core) * half, half, 0)

    def natural(mine, other):
        return jnp.where(
            core == 0, jnp.concatenate([mine, other], 0), jnp.concatenate([other, mine], 0)
        )

    def total_half(mine, other):
        both = mine + swap_core(other)
        return both + swap_x(both)

    def along_z(v, k):
        return lax.ppermute(v, "dp", z_shifts[k])

    def join_x(mine, other):
        return jnp.where(
            x_side == 0, jnp.concatenate([mine, other], 0), jnp.concatenate([other, mine], 0)
        )

    def send_z(split):
        z = dp_place // 2
        place = lambda k: lax.dynamic_index_in_dim(split, (z + k) % 4, 0, False)
        return [place(0)] + [along_z(place(k), k) for k in (1, 2, 3)]

    def split_y(blocks):
        split = blocks.reshape((4, 2) + blocks.shape[1:])
        y = dp_place % 2
        return [lax.dynamic_index_in_dim(split, place, 1, False) for place in (y, 1 - y)]

    def send_y(v):
        return lax.ppermute(v, "dp", y_pairs)

    out_wide = out_grad.astype(wide)
    lane = jnp.arange(EXPERTS, dtype=jnp.int32)
    dense_gates = jnp.sum(
        jnp.where(routes[:, :, None] == lane[None, None, :], gates[:, :, None], 0.0), 1
    )
    quarter = half // 2
    og_mine, og_other = my_half(out_wide), other_half(out_wide)
    gates_mine, gates_other = my_half(dense_gates), other_half(dense_gates)
    shard = width // dp_size

    def my_quarter(v):
        return lax.dynamic_slice_in_dim(v, x_side * quarter, quarter, 0)

    if small:
        og_sent = jnp.concatenate(
            [my_quarter(og_mine), my_quarter(gates_mine).reshape(-1, width)], 0
        )
        og_z = {k: along_z(og_sent, k) for k in (1, 3, 2)}

    tokens_wide = tokens.astype(wide)
    normed1_low = norm_forward(tokens_wide, norm1_gain).astype(bfloat)
    query_proj = dot_nn(normed1_low, w_query)
    key_proj = dot_nn(normed1_low, w_key)
    value_low = (
        dot_nn(normed1_low, w_value).astype(bfloat).reshape(row_count, local_groups, HEAD_DIM)
    )
    cosine, sine_table = rope_tables(positions)

    def turn_query(proj_in):
        return rotate(proj_in.reshape(row_count, local_heads, HEAD_DIM), cosine, sine_table)

    def turn_key(proj_in):
        return rotate(proj_in.reshape(row_count, local_groups, HEAD_DIM), cosine, sine_table)

    query_rot, query_back = jax.vjp(turn_query, query_proj)
    key_rot, key_back = jax.vjp(turn_key, key_proj)
    query_low = query_rot.astype(bfloat).reshape(row_count, local_groups, per_group, HEAD_DIM)
    key_low = key_rot.astype(bfloat)
    key_index = jnp.arange(row_count, dtype=jnp.int32)

    def block_scores(block_num):
        row_start = block_num * block_rows
        query_block = query_low[row_start : row_start + block_rows]
        row_index = row_start + jnp.arange(block_rows, dtype=jnp.int32)
        place_gap = positions[row_start : row_start + block_rows][:, None] - positions[None, :]
        allowed = (row_index[:, None] >= key_index[None, :]) & (
            place_gap == row_index[:, None] - key_index[None, :]
        )
        raw_scores = (
            jnp.einsum("qgrd,kgd->grqk", query_block, key_low, preferred_element_type=wide)
            * scale_factor
        )
        return (jnp.where(allowed[None, None], raw_scores, -1e30), query_block)

    mixed_blocks = []
    log_totals = []
    for block_num in range(block_count):
        scores, query_block = block_scores(block_num)
        row_max = jnp.max(scores, -1, keepdims=True)
        exp_scores = jnp.exp(scores - row_max)
        row_total = jnp.sum(exp_scores, -1, keepdims=True)
        soft_low = (exp_scores / row_total).astype(bfloat)
        log_totals.append(row_max + jnp.log(row_total))
        mixed_blocks.append(
            jnp.einsum("grqk,kgd->qgrd", soft_low, value_low, preferred_element_type=wide)
        )
    mixed_low = (
        jnp.concatenate(mixed_blocks, 0).astype(bfloat).reshape(row_count, local_heads * HEAD_DIM)
    )
    ready = functools.partial(
        prepare,
        gain=norm2_gain,
        place=dp_place if small else jnp.zeros_like(dp_place),
        shard=shard if small else width // 8,
        half=half,
    )
    own_og, own_ogt = ready(og_mine, og_other, normed=False)
    own_gates = jnp.concatenate([gates_mine, gates_other], 0)
    own_back = back_through_down(own_og, w_down)
    if small:
        mixed_low, og_z[1] = together(mixed_low, og_z[1])
    attn_both = dot_nn(my_half(mixed_low), w_out) + swap_core(
        dot_nn(other_half(mixed_low), w_out)
    )
    attention, own_back, own_ogt, own_gates = together(
        attn_both + swap_x(attn_both), own_back, own_ogt, own_gates
    )
    if small:
        attention, og_z[2] = together(attention, og_z[2])
    hidden = my_half(tokens_wide) + attention
    hidden_other = swap_core(hidden)
    weights = (w_gate, w_up)
    own_x, own_xt = ready(hidden, hidden_other, normed=True)
    ga, gu, n_part, n_other = own_experts(own_x, own_back, own_gates, *weights)
    if small:
        z_hidden = {2: along_z(my_quarter(hidden), 2)}
        og_x = {k: swap_x(og_z[k]) for k in (1, 2)}
        n_part, n_other, z_hidden[2], og_x[1], og_x[2] = together(
            n_part, n_other, z_hidden[2], og_x[1], og_x[2]
        )

    n_both = n_part + swap_core(n_other)
    e_mine, e_other = down_products(ga, w_down)
    if small:

        def og_part(k):
            og_h = join_x(og_z[k][:quarter], og_x[k][:quarter])
            gates_h = join_x(og_z[k][quarter:], og_x[k][quarter:])
            og_h = jnp.concatenate([og_h, gates_h], 0)
            arrived = swap_core(og_h)
            prepared = ready(og_h, arrived, normed=False)
            both_gates = jnp.concatenate([gates_h, arrived[half:]], 0).reshape(-1, EXPERTS)
            return [back_through_down(prepared[0], w_down), prepared[1], both_gates]

        n_first = swap_x(n_both[:quarter])
        e_mine, e_other, n_first, og_z[3], og_x[1], og_x[2] = together(
            e_mine, e_other, n_first, og_z[3], og_x[1], og_x[2]
        )
        n_second = swap_x(after(n_both[quarter:], n_first))
        z_first = {1: along_z(after(hidden[:quarter], og_z[3]), 1)}
        og_parts = {2: og_part(2)}
        og_parts[2][0], n_second, og_x[1], z_first[1] = together(
            og_parts[2][0], n_second, og_x[1], z_first[1]
        )
        z_second = {1: along_z(after(hidden[quarter:], z_first[1]), 1)}
        n_arrived = jnp.concatenate([n_first, n_second], 0)
    else:
        n_arrived = swap_x(n_both)
    normed2_grad = n_both + n_arrived
    hidden_part, gain2_grad = norm_backward(hidden, norm2_gain, normed2_grad)
    hidden_grad = my_half(out_wide) + hidden_part
    other_grad = swap_core(hidden_grad)
    attn_grad = natural(hidden_grad.astype(bfloat), rounded(other_grad))
    if small:
        og_x[3] = swap_x(after(og_z[3], n_second))
        hidden_x = swap_x(after(z_hidden[2], n_second))
        og_parts[1] = og_part(1)
        attn_grad, og_parts[1][0], z_second[1] = together(
            attn_grad, og_parts[1][0], z_second[1]
        )
        z_first[3] = along_z(after(hidden[:quarter], z_second[1]), 3)

    mixed_grad = dot_nt(attn_grad, w_out).astype(bfloat)
    mixed_grad = mixed_grad.reshape(row_count, local_groups, per_group, HEAD_DIM)
    key_grad = jnp.zeros((row_count, local_groups, HEAD_DIM), wide)
    value_grad = jnp.zeros((row_count, local_groups, HEAD_DIM), wide)
    query_grads = []
    for block_num in range(block_count):
        row_start = block_num * block_rows
        scores, query_block = block_scores(block_num)
        soft = jnp.exp(scores - log_totals[block_num])
        grad_block = mixed_grad[row_start : row_start + block_rows]
        prob_grad = jnp.einsum("qgrd,kgd->grqk", grad_block, value_low, preferred_element_type=wide)
        row_dot = jnp.sum(soft * prob_grad, -1, keepdims=True)
        score_grad = (soft * (prob_grad - row_dot)).astype(bfloat)
        query_grads.append(
            jnp.einsum("grqk,kgd->qgrd", score_grad, key_low, preferred_element_type=wide)
            * scale_factor
        )
        key_grad = (
            key_grad
            + jnp.einsum("grqk,qgrd->kgd", score_grad, query_block, preferred_element_type=wide)
            * scale_factor
        )
        value_grad = value_grad + jnp.einsum(
            "grqk,qgrd->kgd", soft.astype(bfloat), grad_block, preferred_element_type=wide
        )
    query_rot_grad = jnp.concatenate(query_grads, 0).reshape(row_count, local_heads, HEAD_DIM)
    (query_in,) = query_back(query_rot_grad)
    (key_in,) = key_back(key_grad)
    qkv_low = jnp.concatenate(
        [
            query_in.astype(bfloat),
            key_in.astype(bfloat),
            value_grad.astype(bfloat).reshape(row_count, local_groups * HEAD_DIM),
        ],
        1,
    )
    w_qkv = jnp.concatenate([w_query, w_key, w_value], 1)
    if small:
        qkv_low, og_x[3], hidden_x, z_first[3] = together(
            qkv_low, og_x[3], hidden_x, z_first[3]
        )
        z_second[3] = along_z(after(hidden[quarter:], z_first[3]), 3)
    t_both = dot_nt(my_half(qkv_low), w_qkv) + swap_core(dot_nt(other_half(qkv_low), w_qkv))
    t_arrived = swap_x(t_both)

    def send_expert_part(*start):
        e_both = after(e_mine, *start) + swap_core(after(e_other, *start))
        return e_both, [swap_x(e_both[:quarter]), swap_x(e_both[quarter:])]


    def finish_tokens(t_arrived):
        tokens_part, gain1_grad = norm_backward(
            my_half(tokens_wide), norm1_gain, t_both + t_arrived
        )
        gain1_grad = (gain1_grad + swap_core(gain1_grad)).reshape(dp_size, -1)
        return hidden_grad + tokens_part, gain1_grad

    def join_grads(normed1_low, qkv_low, mixed_low, attn_grad, gain2_grad):
        grad_w_out = jnp.einsum("tc,td->cd", mixed_low, attn_grad, preferred_element_type=wide)
        grad_w_qkv = jnp.einsum("td,tc->dc", normed1_low, qkv_low, preferred_element_type=wide)
        gain2_grad = gain2_grad + swap_core(gain2_grad)
        return jnp.concatenate(
            [
                grad_w_qkv.reshape(dp_size, grad_w_qkv.shape[1], shard),
                grad_w_out.reshape(w_out.shape[0], dp_size, shard).transpose(1, 0, 2),
                jnp.broadcast_to(gain2_grad.reshape(dp_size, 1, shard), (dp_size, 8, shard)),
            ],
            1,
        )

    if small:
        og_parts[3] = og_part(3)
        hidden_parts = {}
        for k in (1, 2, 3):
            if k == 2:
                hidden_h = join_x(z_hidden[2], hidden_x)
            else:
                hidden_h = jnp.concatenate([z_first[k], z_second[k]], 0)
            hidden_parts[k] = list(ready(hidden_h, swap_core(hidden_h), normed=True))
            if k == 2:
                hidden_parts[2][0], z_second[3] = together(hidden_parts[2][0], z_second[3])
        shifts = (1, 2, 3)
        xs = [hidden_parts[k][0] for k in shifts]
        xs = list(lax.optimization_barrier((*xs, t_both))[:3])
        pieces = []
        first = 0
        for number, count in enumerate(CHUNK_SIZES):
            if number == 0:
                joined = split_y(join_grads(normed1_low, qkv_low, mixed_low, attn_grad, gain2_grad))
                *xs, joined[0], joined[1] = together(*xs, *joined)
                joined[1] = send_y(joined[1])
            if number == 1:
                keep, send, joined[1] = together(keep, send, joined[1])
                pieces[0][:2] = keep, send
                joined = send_z(joined[0] + joined[1])
            if number == 2:
                keep, send, t_arrived, *joined, pieces[0][2] = together(
                    keep, send, t_arrived, *joined, pieces[0][2]
                )
                pieces[1][:2] = keep, send
                joined = sum(joined)
                e_both, e_arrived = send_expert_part(keep)
                tokens_half, gain1_grad = finish_tokens(t_arrived)
                *xs, tokens_half, gain1_grad = together(*xs, tokens_half, gain1_grad)
                gain1 = send_z(gain1_grad.reshape(4, 2, -1))
            if number == 3:
                keep, send, e_arrived[0], pieces[1][2], *gain1 = together(
                    keep, send, e_arrived[0], pieces[1][2], *gain1
                )
                pieces[2][:2] = keep, send
                gain1 = sum(gain1)
            keep, send = expert_grads(
                first,
                count,
                xs,
                [og_parts[k][2] for k in shifts],
                [hidden_parts[k][1] for k in shifts],
                [og_parts[k][1] for k in shifts],
                [og_parts[k][0] for k in shifts],
                own_xt,
                own_ogt,
                ga,
                gu,
                weights,
            )
            first += count
            pieces.append([keep, send, send_y(send)])
        keep, e_arrived[1], pieces[2][2] = together(keep, e_arrived[1], pieces[2][2])
        pieces[-1][0] = keep
        block_mine = hidden + (e_both + jnp.concatenate(e_arrived, 0))
        mine_y, other_y = (
            lax.dynamic_index_in_dim(gain1, place, 0, False)
            for place in (dp_place % 2, 1 - dp_place % 2)
        )
        gain1 = mine_y + send_y(other_y)
        block_out = place_halves(block_mine, swap_core(block_mine), core)
        tokens_grad = place_halves(tokens_half, swap_core(tokens_half), core)
        pieces[-1][2], block_out, tokens_grad = together(pieces[-1][2], block_out, tokens_grad)
        grad_w_gate, grad_w_up, grad_w_down = (
            jnp.concatenate([c[0][i] + c[2][i] for c in pieces], 0) for i in range(3)
        )
    else:
        joined = join_grads(normed1_low, qkv_low, mixed_low, attn_grad, gain2_grad)
        joined = lax.psum_scatter(joined, "dp", scatter_dimension=0, tiled=True)[0]
        tokens_half, gain1_grad = finish_tokens(t_arrived)
        gain1 = lax.psum_scatter(gain1_grad, "dp", scatter_dimension=0, tiled=True)[0]
        e_both, e_arrived = send_expert_part(t_both)
        block_mine = hidden + (e_both + jnp.concatenate(e_arrived, 0))
        block_out = place_halves(block_mine, swap_core(block_mine), core)
        tokens_grad = place_halves(tokens_half, swap_core(tokens_half), core)
        ga = ga.transpose(1, 0, 2).reshape(row_count, EXPERTS, -1)
        gu = gu.transpose(1, 0, 2).reshape(row_count, EXPERTS, 2, -1)
        grad_w_gate = jnp.einsum("td,tef->edf", own_x, gu[:, :, 0], preferred_element_type=wide)
        grad_w_up = jnp.einsum("td,tef->edf", own_x, gu[:, :, 1], preferred_element_type=wide)
        grad_w_down = jnp.einsum("tef,td->efd", ga, own_og, preferred_element_type=wide)
        grad_w_gate = lax.psum_scatter(grad_w_gate, "dp", scatter_dimension=1, tiled=True)
        grad_w_up = lax.psum_scatter(grad_w_up, "dp", scatter_dimension=1, tiled=True)
        grad_w_down = lax.psum_scatter(grad_w_down, "dp", scatter_dimension=2, tiled=True)

    qkv_rows = qkv_low.shape[1]
    grad_w_qkv = joined[:qkv_rows].reshape(shard, -1)
    grad_w_out = joined[qkv_rows : qkv_rows + w_out.shape[0]]
    gain2 = joined[-8]
    query_cols, key_cols = w_query.shape[1], w_key.shape[1]
    return (
        block_out,
        tokens_grad,
        gain1,
        grad_w_qkv[:, :query_cols],
        grad_w_qkv[:, query_cols : query_cols + key_cols],
        grad_w_qkv[:, query_cols + key_cols :],
        grad_w_out,
        gain2,
        grad_w_gate,
        grad_w_up,
        grad_w_down,
    )


def solution(mesh):
    placed = (
        P("dp", None),
        P("dp"),
        P("dp", None),
        P("dp", None),
        P(),
        P(None, "tensor"),
        P(None, "tensor"),
        P(None, "tensor"),
        P("tensor", None),
        P(),
        P(None, None, "tensor"),
        P(None, None, "tensor"),
        P(None, "tensor", None),
        P("dp", None),
    )
    return jax.shard_map(
        functools.partial(per_device, mesh.shape["dp"]),
        mesh=mesh,
        in_specs=placed,
        out_specs=(
            P("dp", None),
            P("dp", None),
            P("dp"),
            P("dp", "tensor"),
            P("dp", "tensor"),
            P("dp", "tensor"),
            P("tensor", "dp"),
            P("dp"),
            P(None, "dp", "tensor"),
            P(None, "dp", "tensor"),
            P(None, "tensor", "dp"),
        ),
        check_vma=False,
    )
```

```python
import functools

import jax
import jax.numpy as jnp
from jax import lax
from jax.experimental import pallas as pl
from jax.experimental.pallas import tpu as pltpu
from jax.sharding import PartitionSpec as P

HEAD_DIM = 64
EXPERTS = 32
TOP = 8
EPS = 1e-06
ROPE_BASE = 10000.0
CHUNK_SIZES = (8, 10, 8, 6)

bfloat = jnp.bfloat16
wide = jnp.float32

BRIEF = pl.CostEstimate(flops=2**20, bytes_accessed=2**20, transcendentals=0)

CORE_PAIRS = [(i, i ^ 1) for i in range(4)]
X_PAIRS = [(i, i ^ 2) for i in range(4)]


def dot_nn(a, b):
    return jnp.dot(a, b, preferred_element_type=wide)


def dot_nt(a, b):
    return lax.dot_general(a, b, (((1,), (1,)), ((), ())), preferred_element_type=wide)


def norm_forward(v, gain):
    return v * lax.rsqrt(jnp.mean(v * v, -1, keepdims=True) + EPS) * gain


def norm_backward(v, gain, q):
    r = lax.rsqrt(jnp.mean(v * v, -1, keepdims=True) + EPS)
    gq = gain * q
    v_grad = r * gq - v * (r * r * r) * jnp.mean(v * gq, -1, keepdims=True)
    return v_grad, jnp.sum(q * v * r, 0)


def rope_tables(positions):
    half_dim = HEAD_DIM // 2
    freqs = ROPE_BASE ** (-(jnp.arange(half_dim, dtype=jnp.float32) * 2.0) / HEAD_DIM)
    angles = positions.astype(jnp.float32)[:, None] * freqs[None, :]
    cosine = jnp.cos(angles)
    sine_table = jnp.sin(angles)
    return (jnp.concatenate([cosine, cosine], -1), jnp.concatenate([sine_table, sine_table], -1))


def rotate(values_in, cosine, sine_table):
    half_dim = values_in.shape[-1] // 2
    turned = jnp.concatenate([-values_in[..., half_dim:], values_in[..., :half_dim]], -1)
    return values_in * cosine[:, None, :] + turned * sine_table[:, None, :]


def expert_parts(x, back, gate_cols, w_pair):
    hidden = back.shape[1] // 2
    out = []
    for j in range(2):
        both = dot_nn(x, w_pair[j])
        gate, up = both[:, :hidden], both[:, hidden:]
        col = gate_cols[j]
        sig = 0.5 * jnp.tanh(0.5 * gate) + 0.5
        act = gate * sig
        slope = sig + act * (1.0 - sig)
        weighted = back[:, j * hidden : (j + 1) * hidden].astype(wide) * col
        out.append(
            (
                (act * up * col).astype(bfloat),
                (weighted * up * slope).astype(bfloat),
                (weighted * act).astype(bfloat),
            )
        )
    return out


def gate_columns(g, first):
    lane = lax.broadcasted_iota(jnp.int32, g.shape, 1)
    return [
        jnp.sum(jnp.where(lane == first + j, g, 0.0), axis=1, keepdims=True) for j in range(2)
    ]


def own_body(x_ref, back_ref, g_ref, wg_ref, wu_ref, ga_ref, gu_ref, *n_refs):
    pair = pl.program_id(0)
    hidden = wg_ref.shape[2]

    @pl.when(pair == 0)
    def _():
        for n_ref in n_refs:
            n_ref[...] = jnp.zeros_like(n_ref)

    w_pair = [jnp.concatenate([wg_ref[j], wu_ref[j]], axis=1) for j in range(2)]
    cols = gate_columns(g_ref[...], 2 * pair)
    parts = expert_parts(x_ref[...], back_ref[...], cols, w_pair)
    half = n_refs[0].shape[0]
    totals = [n_ref[...] for n_ref in n_refs]
    for j in range(2):
        ga, gg, ug = parts[j]
        ga_ref[:, j * hidden : (j + 1) * hidden] = ga
        gu = jnp.concatenate([gg, ug], axis=1)
        gu_ref[:, 2 * j * hidden : 2 * (j + 1) * hidden] = gu
        for i in range(2):
            totals[i] = totals[i] + dot_nt(gu[i * half : (i + 1) * half], w_pair[j])
    for n_ref, total in zip(n_refs, totals):
        n_ref[...] = total


def back_body(og_ref, wd_ref, out_ref):
    for i in range(out_ref.shape[0]):
        wd2 = wd_ref[2 * i : 2 * i + 2].reshape(-1, wd_ref.shape[2])
        out_ref[i] = dot_nt(og_ref[...], wd2).astype(bfloat)


def back_through_down(og, w_down):
    rows, width = og.shape
    experts, hidden, _ = w_down.shape
    return pl.pallas_call(
        back_body,
        grid=(experts // 4,),
        in_specs=[whole(og), pl.BlockSpec((4, hidden, width), lambda p: (p, 0, 0))],
        out_specs=pl.BlockSpec((2, rows, 2 * hidden), lambda p: (p, 0, 0)),
        out_shape=jax.ShapeDtypeStruct((experts // 2, rows, 2 * hidden), bfloat),
        compiler_params=pltpu.CompilerParams(
            dimension_semantics=("arbitrary",), vmem_limit_bytes=58 * 2**20
        ),
        cost_estimate=BRIEF,
        name="back_through_down",
    )(og, w_down)


def down_body(ga_ref, wd_ref, *out_refs):
    @pl.when(pl.program_id(0) == 0)
    def _():
        for out_ref in out_refs:
            out_ref[...] = jnp.zeros_like(out_ref)

    wd = wd_ref[...].reshape(-1, wd_ref.shape[2])
    half = out_refs[0].shape[0]
    for i, out_ref in enumerate(out_refs):
        rows = slice(i * half, (i + 1) * half)
        ga = jnp.concatenate([ga_ref[n, rows, :] for n in range(ga_ref.shape[0])], axis=1)
        out_ref[...] += dot_nn(ga, wd)


def down_products(ga, w_down):
    rows = ga.shape[1]
    experts, hidden, width = w_down.shape
    out = jax.ShapeDtypeStruct((rows // 2, width), wide)
    return pl.pallas_call(
        down_body,
        grid=(experts // 4,),
        in_specs=[
            pl.BlockSpec((2, rows, 2 * hidden), lambda p: (p, 0, 0)),
            pl.BlockSpec((4, hidden, width), lambda p: (p, 0, 0)),
        ],
        out_specs=[pl.BlockSpec((rows // 2, width), lambda p: (0, 0))] * 2,
        out_shape=[out, out],
        compiler_params=pltpu.CompilerParams(
            dimension_semantics=("arbitrary",), vmem_limit_bytes=58 * 2**20
        ),
        cost_estimate=BRIEF,
        name="down_products",
    )(ga, w_down)


def whole(a):
    return pl.BlockSpec(a.shape, lambda *_: (0,) * a.ndim, pipeline_mode=pl.Buffered(1))


def own_experts(x, back, g, w_gate, w_up):
    rows, width = x.shape
    experts, _, hidden = w_gate.shape
    up_spec = pl.BlockSpec((2, width, hidden), lambda p: (p, 0, 0))
    return pl.pallas_call(
        own_body,
        grid=(experts // 2,),
        in_specs=[
            whole(x),
            pl.BlockSpec((None, rows, 2 * hidden), lambda p: (p, 0, 0)),
            whole(g),
            up_spec,
            up_spec,
        ],
        out_specs=[
            pl.BlockSpec((None, rows, 2 * hidden), lambda p: (p, 0, 0)),
            pl.BlockSpec((None, rows, 4 * hidden), lambda p: (p, 0, 0)),
            pl.BlockSpec((rows // 2, width), lambda p: (0, 0)),
            pl.BlockSpec((rows // 2, width), lambda p: (0, 0)),
        ],
        out_shape=[
            jax.ShapeDtypeStruct((experts // 2, rows, 2 * hidden), bfloat),
            jax.ShapeDtypeStruct((experts // 2, rows, 4 * hidden), bfloat),
            jax.ShapeDtypeStruct((rows // 2, width), wide),
            jax.ShapeDtypeStruct((rows // 2, width), wide),
        ],
        compiler_params=pltpu.CompilerParams(
            dimension_semantics=("arbitrary",), vmem_limit_bytes=40 * 2**20
        ),
        cost_estimate=BRIEF,
        name="own_experts",
    )(x, back, g, w_gate, w_up)


def grads_body(first, parts_n, *refs):
    x_refs, g_refs, xt_refs, ogt_refs, back_refs = (
        refs[parts_n * i : parts_n * (i + 1)] for i in range(5)
    )
    own_xt, own_ogt, own_ga, own_gu, wg_ref, wu_ref, keep, send = refs[
        5 * parts_n : 5 * parts_n + 8
    ]
    s_refs, sa_ref = refs[-3:-1], refs[-1]
    pair = pl.program_id(0)
    hidden = wg_ref.shape[2]
    w_pair = [jnp.concatenate([wg_ref[j], wu_ref[j]], axis=1) for j in range(2)]
    rows = x_refs[0].shape[0]

    for n in range(parts_n):
        to = slice(n * rows, (n + 1) * rows)
        cols = gate_columns(g_refs[n][...], 2 * (pair + first))
        parts = expert_parts(x_refs[n][...], back_refs[n][...], cols, w_pair)
        for j in range(2):
            ga, gg, ug = parts[j]
            sa_ref[to, j * hidden : (j + 1) * hidden] = ga
            s_refs[j][to, :hidden] = gg
            s_refs[j][to, hidden:] = ug

    def total(transposed, own_transposed, scratch, own):
        out = dot_nn(own_transposed[...], own)
        for n in range(parts_n):
            out = out + dot_nn(transposed[n][...], scratch[n * rows : (n + 1) * rows])
        return out

    shard = own_xt.shape[0] // 2
    for j in range(2):
        lanes = slice(2 * j * hidden, 2 * (j + 1) * hidden)
        grad = total(xt_refs, own_xt, s_refs[j], own_gu[:, lanes])
        for i in range(2):
            keep[i, j] = grad[:shard, i * hidden : (i + 1) * hidden]
            send[i, j] = grad[shard:, i * hidden : (i + 1) * hidden]
    down = total(ogt_refs, own_ogt, sa_ref, own_ga[...])
    for j in range(2):
        turned = down[:, j * hidden : (j + 1) * hidden].T
        keep[2, j] = turned[:, :shard]
        send[2, j] = turned[:, shard:]


def expert_grads(first_expert, count, x, g, xt, ogt, back, own_xt, own_ogt, own_ga, own_gu, weights):
    rows, width = x[0].shape
    w_gate, w_up = weights
    _, _, hidden = w_gate.shape
    own_rows = own_ga.shape[1]
    all_rows = len(x) * rows
    shard = own_xt.shape[0] // 2
    first = first_expert // 2
    up_spec = pl.BlockSpec((2, width, hidden), lambda p: (p + first, 0, 0))
    out_spec = pl.BlockSpec((3, 2, shard, hidden), lambda p: (0, p, 0, 0))
    out_shape = jax.ShapeDtypeStruct((3, count, shard, hidden), wide)
    resident = (*x, *g, *xt, *ogt)
    pair_spec = lambda n: pl.BlockSpec((None, n, 2 * hidden), lambda p: (p + first, 0, 0))
    return pl.pallas_call(
        functools.partial(grads_body, first, len(x)),
        grid=(count // 2,),
        in_specs=[whole(a) for a in resident]
        + [pair_spec(rows)] * len(back)
        + [whole(own_xt), whole(own_ogt), pair_spec(own_rows)]
        + [pl.BlockSpec((None, own_rows, 4 * hidden), lambda p: (p + first, 0, 0))]
        + [up_spec, up_spec],
        out_specs=[out_spec] * 2,
        out_shape=[out_shape] * 2,
        scratch_shapes=[pltpu.VMEM((all_rows, 2 * hidden), bfloat)] * 3,
        compiler_params=pltpu.CompilerParams(
            dimension_semantics=("arbitrary",), vmem_limit_bytes=48 * 2**20
        ),
        cost_estimate=pl.CostEstimate(
            flops=count * 2**32, bytes_accessed=count * 2**22, transcendentals=0
        ),
        name="expert_grads",
    )(*resident, *back, own_xt, own_ogt, own_ga, own_gu, *weights)


def prepare_body(normed, place_ref, mine_ref, other_ref, gain_ref, x_ref, t_ref):
    shard = t_ref.shape[0] // 2
    blocks = pl.num_programs(0) // 2

    def emit(v_ref):
        v = v_ref[...]
        if normed:
            scale = lax.rsqrt(jnp.mean(v * v, -1, keepdims=True) + EPS)
            v = v * scale * gain_ref[...]
        x_ref[...] = v.astype(bfloat)
        for i in range(2):
            cols = pl.ds(pl.multiple_of((place_ref[0] ^ i) * shard, shard), shard)
            cut = v_ref[:, cols]
            if normed:
                cut = cut * scale * gain_ref[:, cols]
            t_ref[i * shard : (i + 1) * shard, :] = cut.T.astype(bfloat)

    @pl.when(pl.program_id(0) < blocks)
    def _():
        emit(mine_ref)

    @pl.when(pl.program_id(0) >= blocks)
    def _():
        emit(other_ref)


def prepare(mine, other, gain, place, shard, half, normed):
    width = mine.shape[1]
    block = 256
    blocks = half // block
    return pl.pallas_call(
        functools.partial(prepare_body, normed),
        grid_spec=pltpu.PrefetchScalarGridSpec(
            num_scalar_prefetch=1,
            grid=(2 * blocks,),
            in_specs=[
                pl.BlockSpec((block, width), lambda i, _: (jnp.minimum(i, blocks - 1), 0)),
                pl.BlockSpec((block, width), lambda i, _: (jnp.maximum(i - blocks, 0), 0)),
                pl.BlockSpec((1, width), lambda i, _: (0, 0)),
            ],
            out_specs=[
                pl.BlockSpec((block, width), lambda i, _: (i, 0)),
                pl.BlockSpec((2 * shard, block), lambda i, _: (0, i)),
            ],
        ),
        out_shape=[
            jax.ShapeDtypeStruct((2 * half, width), bfloat),
            jax.ShapeDtypeStruct((2 * shard, 2 * half), bfloat),
        ],
        cost_estimate=BRIEF,
        name="prepare",
    )(place.reshape(1), mine, other, gain.reshape(1, width))


def place_halves_body(core_ref, mine_ref, other_ref, out_ref):
    half = pl.program_id(0)

    @pl.when(half == 0)
    def _():
        out_ref[...] = mine_ref[...]

    @pl.when(half == 1)
    def _():
        out_ref[...] = other_ref[...]


def place_halves(mine, other, core):
    rows, width = mine.shape
    steps = 2
    block = (rows // steps, width)
    return pl.pallas_call(
        place_halves_body,
        grid_spec=pltpu.PrefetchScalarGridSpec(
            num_scalar_prefetch=1,
            grid=(2, steps),
            in_specs=[
                pl.BlockSpec(block, lambda h, i, _: (jnp.where(h == 0, i, steps - 1), 0)),
                pl.BlockSpec(block, lambda h, i, _: (jnp.where(h == 0, 0, i), 0)),
            ],
            out_specs=pl.BlockSpec(block, lambda h, i, c: ((h ^ c[0]) * steps + i, 0)),
        ),
        out_shape=jax.ShapeDtypeStruct((2 * rows, width), mine.dtype),
        cost_estimate=BRIEF,
        name="place_halves",
    )(core.reshape(1), mine, other)


def after(v, *others):
    return lax.optimization_barrier((v, *others))[0]


def together(*values):
    return lax.optimization_barrier(values)


def per_device(
    dp_size,
    tokens,
    positions,
    routes,
    gates,
    norm1_gain,
    w_query,
    w_key,
    w_value,
    w_out,
    norm2_gain,
    w_gate,
    w_up,
    w_down,
    out_grad,
):
    row_count, width = tokens.shape
    half = row_count // 2
    local_heads = w_query.shape[1] // HEAD_DIM
    local_groups = w_key.shape[1] // HEAD_DIM
    per_group = local_heads // local_groups
    scale_factor = HEAD_DIM ** (-0.5)
    block_rows = min(512, row_count)
    block_count = row_count // block_rows
    core = lax.axis_index("tensor") % 2
    x_side = lax.axis_index("tensor") // 2
    dp_place = lax.axis_index("dp")
    small = dp_size == 8
    z_shifts = {k: [(i, (i + 2 * k) % 8) for i in range(8)] for k in (1, 2, 3)}
    y_pairs = [(i, i ^ 1) for i in range(dp_size)]

    one = jnp.where(dp_place < 0, 0.5, 1.0).astype(wide)

    def rounded(v):
        return (v * one).astype(bfloat)

    def swap_core(v):
        return lax.ppermute(v, "tensor", CORE_PAIRS)

    def swap_x(v):
        return lax.ppermute(v, "tensor", X_PAIRS)

    def my_half(v):
        return lax.dynamic_slice_in_dim(v, core * half, half, 0)

    def other_half(v):
        return lax.dynamic_slice_in_dim(v, (1 - core) * half, half, 0)

    def natural(mine, other):
        return jnp.where(
            core == 0, jnp.concatenate([mine, other], 0), jnp.concatenate([other, mine], 0)
        )

    def total_half(mine, other):
        both = mine + swap_core(other)
        return both + swap_x(both)

    def along_z(v, k):
        return lax.ppermute(v, "dp", z_shifts[k])

    def join_x(mine, other):
        return jnp.where(
            x_side == 0, jnp.concatenate([mine, other], 0), jnp.concatenate([other, mine], 0)
        )

    def send_z(split):
        z = dp_place // 2
        place = lambda k: lax.dynamic_index_in_dim(split, (z + k) % 4, 0, False)
        return [place(0)] + [along_z(place(k), k) for k in (1, 2, 3)]

    def split_y(blocks):
        split = blocks.reshape((4, 2) + blocks.shape[1:])
        y = dp_place % 2
        return [lax.dynamic_index_in_dim(split, place, 1, False) for place in (y, 1 - y)]

    def send_y(v):
        return lax.ppermute(v, "dp", y_pairs)

    out_wide = out_grad.astype(wide)
    lane = jnp.arange(EXPERTS, dtype=jnp.int32)
    dense_gates = jnp.sum(
        jnp.where(routes[:, :, None] == lane[None, None, :], gates[:, :, None], 0.0), 1
    )
    quarter = half // 2
    og_mine, og_other = my_half(out_wide), other_half(out_wide)
    gates_mine, gates_other = my_half(dense_gates), other_half(dense_gates)
    shard = width // dp_size

    def my_quarter(v):
        return lax.dynamic_slice_in_dim(v, x_side * quarter, quarter, 0)

    if small:
        og_sent = jnp.concatenate(
            [my_quarter(og_mine), my_quarter(gates_mine).reshape(-1, width)], 0
        )
        og_z = {k: along_z(og_sent, k) for k in (1, 3, 2)}

    tokens_wide = tokens.astype(wide)
    normed1_low = norm_forward(tokens_wide, norm1_gain).astype(bfloat)
    query_proj = dot_nn(normed1_low, w_query)
    key_proj = dot_nn(normed1_low, w_key)
    value_low = (
        dot_nn(normed1_low, w_value).astype(bfloat).reshape(row_count, local_groups, HEAD_DIM)
    )
    cosine, sine_table = rope_tables(positions)

    def turn_query(proj_in):
        return rotate(proj_in.reshape(row_count, local_heads, HEAD_DIM), cosine, sine_table)

    def turn_key(proj_in):
        return rotate(proj_in.reshape(row_count, local_groups, HEAD_DIM), cosine, sine_table)

    query_rot, query_back = jax.vjp(turn_query, query_proj)
    key_rot, key_back = jax.vjp(turn_key, key_proj)
    query_low = query_rot.astype(bfloat).reshape(row_count, local_groups, per_group, HEAD_DIM)
    key_low = key_rot.astype(bfloat)
    key_index = jnp.arange(row_count, dtype=jnp.int32)

    def block_scores(block_num):
        row_start = block_num * block_rows
        query_block = query_low[row_start : row_start + block_rows]
        row_index = row_start + jnp.arange(block_rows, dtype=jnp.int32)
        place_gap = positions[row_start : row_start + block_rows][:, None] - positions[None, :]
        allowed = (row_index[:, None] >= key_index[None, :]) & (
            place_gap == row_index[:, None] - key_index[None, :]
        )
        raw_scores = (
            jnp.einsum("qgrd,kgd->grqk", query_block, key_low, preferred_element_type=wide)
            * scale_factor
        )
        return (jnp.where(allowed[None, None], raw_scores, -1e30), query_block)

    mixed_blocks = []
    log_totals = []
    for block_num in range(block_count):
        scores, query_block = block_scores(block_num)
        row_max = jnp.max(scores, -1, keepdims=True)
        exp_scores = jnp.exp(scores - row_max)
        row_total = jnp.sum(exp_scores, -1, keepdims=True)
        soft_low = (exp_scores / row_total).astype(bfloat)
        log_totals.append(row_max + jnp.log(row_total))
        mixed_blocks.append(
            jnp.einsum("grqk,kgd->qgrd", soft_low, value_low, preferred_element_type=wide)
        )
    mixed_low = (
        jnp.concatenate(mixed_blocks, 0).astype(bfloat).reshape(row_count, local_heads * HEAD_DIM)
    )
    ready = functools.partial(
        prepare,
        gain=norm2_gain,
        place=dp_place if small else jnp.zeros_like(dp_place),
        shard=shard if small else width // 8,
        half=half,
    )
    own_og, own_ogt = ready(og_mine, og_other, normed=False)
    own_gates = jnp.concatenate([gates_mine, gates_other], 0)
    own_back = back_through_down(own_og, w_down)
    if small:
        mixed_low, og_z[1] = together(mixed_low, og_z[1])
    attn_both = dot_nn(my_half(mixed_low), w_out) + swap_core(
        dot_nn(other_half(mixed_low), w_out)
    )
    attention, own_back, own_ogt, own_gates = together(
        attn_both + swap_x(attn_both), own_back, own_ogt, own_gates
    )
    if small:
        attention, og_z[2] = together(attention, og_z[2])
    hidden = my_half(tokens_wide) + attention
    hidden_other = swap_core(hidden)
    weights = (w_gate, w_up)
    own_x, own_xt = ready(hidden, hidden_other, normed=True)
    ga, gu, n_part, n_other = own_experts(own_x, own_back, own_gates, *weights)
    if small:
        z_hidden = {2: along_z(my_quarter(hidden), 2)}
        og_x = {k: swap_x(og_z[k]) for k in (1, 2)}
        n_part, n_other, z_hidden[2], og_x[1], og_x[2] = together(
            n_part, n_other, z_hidden[2], og_x[1], og_x[2]
        )

    n_both = n_part + swap_core(n_other)
    e_mine, e_other = down_products(ga, w_down)
    if small:

        def og_part(k):
            og_h = join_x(og_z[k][:quarter], og_x[k][:quarter])
            gates_h = join_x(og_z[k][quarter:], og_x[k][quarter:])
            og_h = jnp.concatenate([og_h, gates_h], 0)
            arrived = swap_core(og_h)
            prepared = ready(og_h, arrived, normed=False)
            both_gates = jnp.concatenate([gates_h, arrived[half:]], 0).reshape(-1, EXPERTS)
            return [back_through_down(prepared[0], w_down), prepared[1], both_gates]

        n_first = swap_x(n_both[:quarter])
        e_mine, e_other, n_first, og_z[3], og_x[1], og_x[2] = together(
            e_mine, e_other, n_first, og_z[3], og_x[1], og_x[2]
        )
        n_second = swap_x(after(n_both[quarter:], n_first))
        z_first = {1: along_z(after(hidden[:quarter], og_z[3]), 1)}
        og_parts = {2: og_part(2)}
        og_parts[2][0], n_second, og_x[1], z_first[1] = together(
            og_parts[2][0], n_second, og_x[1], z_first[1]
        )
        z_second = {1: along_z(after(hidden[quarter:], z_first[1]), 1)}
        n_arrived = jnp.concatenate([n_first, n_second], 0)
    else:
        n_arrived = swap_x(n_both)
    normed2_grad = n_both + n_arrived
    hidden_part, gain2_grad = norm_backward(hidden, norm2_gain, normed2_grad)
    hidden_grad = my_half(out_wide) + hidden_part
    other_grad = swap_core(hidden_grad)
    attn_grad = natural(hidden_grad.astype(bfloat), rounded(other_grad))
    if small:
        og_x[3] = swap_x(after(og_z[3], n_second))
        hidden_x = swap_x(after(z_hidden[2], n_second))
        og_parts[1] = og_part(1)
        attn_grad, og_parts[1][0], z_second[1] = together(
            attn_grad, og_parts[1][0], z_second[1]
        )
        z_first[3] = along_z(after(hidden[:quarter], z_second[1]), 3)

    mixed_grad = dot_nt(attn_grad, w_out).astype(bfloat)
    mixed_grad = mixed_grad.reshape(row_count, local_groups, per_group, HEAD_DIM)
    key_grad = jnp.zeros((row_count, local_groups, HEAD_DIM), wide)
    value_grad = jnp.zeros((row_count, local_groups, HEAD_DIM), wide)
    query_grads = []
    for block_num in range(block_count):
        row_start = block_num * block_rows
        scores, query_block = block_scores(block_num)
        soft = jnp.exp(scores - log_totals[block_num])
        grad_block = mixed_grad[row_start : row_start + block_rows]
        prob_grad = jnp.einsum("qgrd,kgd->grqk", grad_block, value_low, preferred_element_type=wide)
        row_dot = jnp.sum(soft * prob_grad, -1, keepdims=True)
        score_grad = (soft * (prob_grad - row_dot)).astype(bfloat)
        query_grads.append(
            jnp.einsum("grqk,kgd->qgrd", score_grad, key_low, preferred_element_type=wide)
            * scale_factor
        )
        key_grad = (
            key_grad
            + jnp.einsum("grqk,qgrd->kgd", score_grad, query_block, preferred_element_type=wide)
            * scale_factor
        )
        value_grad = value_grad + jnp.einsum(
            "grqk,qgrd->kgd", soft.astype(bfloat), grad_block, preferred_element_type=wide
        )
    query_rot_grad = jnp.concatenate(query_grads, 0).reshape(row_count, local_heads, HEAD_DIM)
    (query_in,) = query_back(query_rot_grad)
    (key_in,) = key_back(key_grad)
    qkv_low = jnp.concatenate(
        [
            query_in.astype(bfloat),
            key_in.astype(bfloat),
            value_grad.astype(bfloat).reshape(row_count, local_groups * HEAD_DIM),
        ],
        1,
    )
    w_qkv = jnp.concatenate([w_query, w_key, w_value], 1)
    if small:
        qkv_low, og_x[3], hidden_x, z_first[3] = together(
            qkv_low, og_x[3], hidden_x, z_first[3]
        )
        z_second[3] = along_z(after(hidden[quarter:], z_first[3]), 3)
    t_both = dot_nt(my_half(qkv_low), w_qkv) + swap_core(dot_nt(other_half(qkv_low), w_qkv))
    t_arrived = swap_x(t_both)

    def send_expert_part(*start):
        e_both = after(e_mine, *start) + swap_core(after(e_other, *start))
        first = swap_x(e_both[:quarter])
        return e_both, [first, swap_x(after(e_both[quarter:], first))]


    def finish_tokens(t_arrived):
        tokens_part, gain1_grad = norm_backward(
            my_half(tokens_wide), norm1_gain, t_both + t_arrived
        )
        gain1_grad = (gain1_grad + swap_core(gain1_grad)).reshape(dp_size, -1)
        return hidden_grad + tokens_part, gain1_grad

    def join_grads(normed1_low, qkv_low, mixed_low, attn_grad, gain2_grad):
        grad_w_out = jnp.einsum("tc,td->cd", mixed_low, attn_grad, preferred_element_type=wide)
        grad_w_qkv = jnp.einsum("td,tc->dc", normed1_low, qkv_low, preferred_element_type=wide)
        gain2_grad = gain2_grad + swap_core(gain2_grad)
        return jnp.concatenate(
            [
                grad_w_qkv.reshape(dp_size, grad_w_qkv.shape[1], shard),
                grad_w_out.reshape(w_out.shape[0], dp_size, shard).transpose(1, 0, 2),
                jnp.broadcast_to(gain2_grad.reshape(dp_size, 1, shard), (dp_size, 8, shard)),
            ],
            1,
        )

    if small:
        og_parts[3] = og_part(3)
        hidden_parts = {}
        for k in (1, 2, 3):
            if k == 2:
                hidden_h = join_x(z_hidden[2], hidden_x)
            else:
                hidden_h = jnp.concatenate([z_first[k], z_second[k]], 0)
            hidden_parts[k] = list(ready(hidden_h, swap_core(hidden_h), normed=True))
            if k == 2:
                hidden_parts[2][0], z_second[3] = together(hidden_parts[2][0], z_second[3])
        shifts = (1, 2, 3)
        xs = [hidden_parts[k][0] for k in shifts]
        xs = list(lax.optimization_barrier((*xs, t_both))[:3])
        pieces = []
        first = 0
        for number, count in enumerate(CHUNK_SIZES):
            if number == 0:
                joined = split_y(join_grads(normed1_low, qkv_low, mixed_low, attn_grad, gain2_grad))
                *xs, joined[0], joined[1] = together(*xs, *joined)
                joined[1] = send_y(joined[1])
            if number == 1:
                keep, send, t_arrived, joined[1] = together(keep, send, t_arrived, joined[1])
                pieces[0][:2] = keep, send
                joined = send_z(joined[0] + joined[1])
                e_both = after(e_mine, keep) + swap_core(after(e_other, keep))
                e_first = swap_x(e_both[:quarter])
            if number == 2:
                keep, send, t_arrived, e_first, pieces[0][2], *joined = together(
                    keep, send, t_arrived, e_first, pieces[0][2], *joined
                )
                pieces[1][:2] = keep, send
                joined = sum(joined)
                e_second = swap_x(after(e_both[quarter:], e_first))
                tokens_half, gain1_grad = finish_tokens(t_arrived)
                *xs, tokens_half, gain1_grad = together(*xs, tokens_half, gain1_grad)
                gain1 = send_z(gain1_grad.reshape(4, 2, -1))
            if number == 3:
                keep, send, e_second, pieces[1][2], *gain1 = together(
                    keep, send, e_second, pieces[1][2], *gain1
                )
                pieces[2][:2] = keep, send
                gain1 = sum(gain1)
                block_mine = hidden + (e_both + jnp.concatenate([e_first, e_second], 0))
                block_out = place_halves(block_mine, swap_core(block_mine), core)
                tokens_grad = place_halves(tokens_half, swap_core(tokens_half), core)
                *xs, block_out, tokens_grad = together(*xs, block_out, tokens_grad)
            keep, send = expert_grads(
                first,
                count,
                xs,
                [og_parts[k][2] for k in shifts],
                [hidden_parts[k][1] for k in shifts],
                [og_parts[k][1] for k in shifts],
                [og_parts[k][0] for k in shifts],
                own_xt,
                own_ogt,
                ga,
                gu,
                weights,
            )
            first += count
            pieces.append([keep, send, send_y(send)])
        keep, pieces[2][2] = together(keep, pieces[2][2])
        pieces[-1][0] = keep
        mine_y, other_y = (
            lax.dynamic_index_in_dim(gain1, place, 0, False)
            for place in (dp_place % 2, 1 - dp_place % 2)
        )
        gain1 = mine_y + send_y(other_y)
        grad_w_gate, grad_w_up, grad_w_down = (
            jnp.concatenate([c[0][i] + c[2][i] for c in pieces], 0) for i in range(3)
        )
    else:
        joined = join_grads(normed1_low, qkv_low, mixed_low, attn_grad, gain2_grad)
        joined = lax.psum_scatter(joined, "dp", scatter_dimension=0, tiled=True)[0]
        tokens_half, gain1_grad = finish_tokens(t_arrived)
        gain1 = lax.psum_scatter(gain1_grad, "dp", scatter_dimension=0, tiled=True)[0]
        e_both, e_arrived = send_expert_part(t_both)
        block_mine = hidden + (e_both + jnp.concatenate(e_arrived, 0))
        block_out = place_halves(block_mine, swap_core(block_mine), core)
        tokens_grad = place_halves(tokens_half, swap_core(tokens_half), core)
        ga = ga.transpose(1, 0, 2).reshape(row_count, EXPERTS, -1)
        gu = gu.transpose(1, 0, 2).reshape(row_count, EXPERTS, 2, -1)
        grad_w_gate = jnp.einsum("td,tef->edf", own_x, gu[:, :, 0], preferred_element_type=wide)
        grad_w_up = jnp.einsum("td,tef->edf", own_x, gu[:, :, 1], preferred_element_type=wide)
        grad_w_down = jnp.einsum("tef,td->efd", ga, own_og, preferred_element_type=wide)
        grad_w_gate = lax.psum_scatter(grad_w_gate, "dp", scatter_dimension=1, tiled=True)
        grad_w_up = lax.psum_scatter(grad_w_up, "dp", scatter_dimension=1, tiled=True)
        grad_w_down = lax.psum_scatter(grad_w_down, "dp", scatter_dimension=2, tiled=True)

    qkv_rows = qkv_low.shape[1]
    grad_w_qkv = joined[:qkv_rows].reshape(shard, -1)
    grad_w_out = joined[qkv_rows : qkv_rows + w_out.shape[0]]
    gain2 = joined[-8]
    query_cols, key_cols = w_query.shape[1], w_key.shape[1]
    return (
        block_out,
        tokens_grad,
        gain1,
        grad_w_qkv[:, :query_cols],
        grad_w_qkv[:, query_cols : query_cols + key_cols],
        grad_w_qkv[:, query_cols + key_cols :],
        grad_w_out,
        gain2,
        grad_w_gate,
        grad_w_up,
        grad_w_down,
    )


def solution(mesh):
    placed = (
        P("dp", None),
        P("dp"),
        P("dp", None),
        P("dp", None),
        P(),
        P(None, "tensor"),
        P(None, "tensor"),
        P(None, "tensor"),
        P("tensor", None),
        P(),
        P(None, None, "tensor"),
        P(None, None, "tensor"),
        P(None, "tensor", None),
        P("dp", None),
    )
    return jax.shard_map(
        functools.partial(per_device, mesh.shape["dp"]),
        mesh=mesh,
        in_specs=placed,
        out_specs=(
            P("dp", None),
            P("dp", None),
            P("dp"),
            P("dp", "tensor"),
            P("dp", "tensor"),
            P("dp", "tensor"),
            P("tensor", "dp"),
            P("dp"),
            P(None, "dp", "tensor"),
            P(None, "dp", "tensor"),
            P(None, "tensor", "dp"),
        ),
        check_vma=False,
    )
```
